256 devices in a mesh: group: 16 (over z, core), mode: 16 (over y, x).
Axes of the slice: x: 4, y: 4, z: 8, core: 2. Of those that a mesh axis runs over, the one named last changes fastest.
Arguments:
- shapes: bfloat16 [2, 16, 512, 2048], P(None, 'group', None, 'mode'), may hold values from -0.75 to 0.75
- pairs: int32 [16, 2], P('group'), may hold values from 0 to 15
- omega: float32 [2048], P('mode'), may hold values from 0.5 to 4
- damping: float32 [2048], P('mode'), may hold values from 0.02 to 0.2
- speeds: float32 [4], replicated, may hold values from 0.6 to 3
Outputs:
- receptance: float32 [512, 16, 4, 2, 512], P('mode', 'group')
The draws below stay inside these ranges and needn't reach their ends.
All inputs are finite; a program needn't handle non-finite values.
Results may differ from the reference program's by a relative error of at most 0.0029.
Values may be sent and summed in bfloat16 or wider, within the bound.
No kernel may reach another device: no remote copies, remote signals or barrier semaphores. Data moves between devices by JAX's collectives and lax.ppermute only.
A program may use at most 64 MiB of HBM per device.

```python
import math
import jax
import jax.numpy as jnp
from jax import lax

RDOF = 512
MODES = 2048
SPEEDS = 4
PAIRS = 16
REG = 16


def plant(drawn, key, smallest, high):
    dims = drawn.shape
    spot = [jax.random.randint(jax.random.fold_in(key, axis), (), 0, dims[axis]) for axis in range(len(dims))]
    drawn = drawn.at[tuple(spot)].set(smallest)
    longest = dims.index(max(dims))
    spot[longest] = (spot[longest] + 1) % dims[longest]
    return drawn.at[tuple(spot)].set(high)


def steps_of(own_key, shape, split, smallest, high):
    def one(axis_at, parts):
        steps = jax.random.uniform(jax.random.fold_in(jax.random.fold_in(own_key, 6), axis_at), (parts,), jnp.float32, smallest / len(split), high / len(split))
        return jnp.repeat(jnp.exp(steps), shape[axis_at] // parts).reshape((-1,) + (1,) * (len(shape) - axis_at - 1))

    factor_of = one(*split[0])
    for cut in split[1:]:
        factor_of = factor_of * one(*cut)
    return factor_of


def normal_values(own_key, extent, spread, reach, split=(), kind=jnp.bfloat16):
    gain = steps_of(own_key, extent, split, -0.22, 0.18) if split else 1.0
    array = jax.random.normal(own_key, extent, jnp.float32) * spread * gain
    return jnp.minimum(jnp.maximum(array, -reach), reach).astype(kind)


def setup_inputs(seed: int = 0) -> dict:
    arg_keys = jax.random.split(jax.random.key(seed), 6)
    shapes = normal_values(arg_keys[0], (2, REG, RDOF, MODES), 64 ** -0.5, 0.75, ((1, 16), (3, 16)))
    pairs = plant(jax.random.randint(arg_keys[1], (PAIRS, 2), 0, REG), jax.random.fold_in(arg_keys[1], 1), 0, REG - 1).astype(jnp.int32)
    omega = jnp.clip(jnp.exp(math.log(4.0) - 2.0794415 * jax.random.uniform(arg_keys[2], (MODES,), jnp.float32) ** steps_of(arg_keys[2], (MODES,), ((0, 16),), -0.2, 0.2)), 0.5, 4.0)
    damping = jnp.clip(jnp.exp(math.log(0.2) - 2.3025851 * jax.random.uniform(arg_keys[3], (MODES,), jnp.float32) ** steps_of(arg_keys[3], (MODES,), ((0, 16),), -0.2, 0.2)), 0.02, 0.2)
    speeds = jnp.clip(jax.random.uniform(arg_keys[4], (SPEEDS,), jnp.float32, 0.6, 3.0), 0.6, 3.0)
    return dict(shapes=shapes, pairs=pairs, omega=omega, damping=damping, speeds=speeds)


def modal_weights(omega, damping, speeds):
    real_part = omega[None, :] ** 2 - speeds[:, None] ** 2
    imag_part = 2.0 * damping[None, :] * omega[None, :] * speeds[:, None]
    denom = real_part * real_part + imag_part * imag_part
    return real_part / denom, -imag_part / denom


def one_pair(shapes, pair_row, weight_re, weight_im):
    response = lax.dynamic_index_in_dim(shapes, pair_row[0].astype(jnp.int32), 1, keepdims=False)
    excite = lax.dynamic_index_in_dim(shapes, pair_row[1].astype(jnp.int32), 1, keepdims=False)
    excite_re = excite[0].astype(jnp.float32)[None]
    excite_im = excite[1].astype(jnp.float32)[None]
    loaded_re = (weight_re[:, None, :] * excite_re - weight_im[:, None, :] * excite_im).astype(jnp.bfloat16)
    loaded_im = (weight_re[:, None, :] * excite_im + weight_im[:, None, :] * excite_re).astype(jnp.bfloat16)
    resp_re = response[0].astype(jnp.float32)
    resp_im = response[1].astype(jnp.float32)
    lre = loaded_re.astype(jnp.float32)
    lim = loaded_im.astype(jnp.float32)
    out_re = jnp.einsum('km,sjm->sjk', resp_re, lre) - jnp.einsum('km,sjm->sjk', resp_im, lim)
    out_im = jnp.einsum('km,sjm->sjk', resp_re, lim) + jnp.einsum('km,sjm->sjk', resp_im, lre)
    return jnp.stack([out_re, out_im], axis=1)


def reference(shapes, pairs, omega, damping, speeds):
    weight_re, weight_im = modal_weights(omega, damping, speeds)
    blocks = lax.map(lambda pair_row: one_pair(shapes, pair_row, weight_re, weight_im), pairs)
    return jnp.transpose(blocks, (4, 0, 1, 2, 3))
```

```python
import jax
import jax.numpy as jnp
from jax import lax
from jax.experimental import pallas as pl
from jax.experimental.pallas import tpu as pltpu
from jax.sharding import PartitionSpec as P

BF = jnp.bfloat16
F32 = jnp.float32
VMEM = pl.BlockSpec(memory_space=pltpu.VMEM)
SMEM = pl.BlockSpec(memory_space=pltpu.SMEM)
PARAMS = pltpu.CompilerParams(vmem_limit_bytes=40 * 1024 * 1024)


def call(kernel, out_shape, in_specs, name, scratch=()):
    return pl.pallas_call(
        kernel,
        out_shape=out_shape,
        in_specs=in_specs,
        out_specs=VMEM,
        scratch_shapes=list(scratch),
        compiler_params=PARAMS,
        name=name,
    )


def slice_kernel(shapes_ref, pairs_ref, out_ref):
    rows = lax.broadcasted_iota(jnp.int32, (16, 128), 0)
    pair = jnp.where(rows < 8, pairs_ref[0, 0], pairs_ref[0, 1])
    pair = pair.astype(F32).astype(BF)
    for i in range(16):
        out_ref[i, 0:32, :] = shapes_ref[0, 0, 32 * i : 32 * i + 32, :]
        out_ref[i, 32:64, :] = shapes_ref[1, 0, 32 * i : 32 * i + 32, :]
        out_ref[i, 64:80, :] = pair


def pick_kernel(all_ref, out_ref):
    for g in range(16):
        pair = all_ref[g, 64:80, :].astype(F32)
        response = pair[0, 0].astype(jnp.int32)
        excite = pair[8, 0].astype(jnp.int32)
        out_ref[g, 0:64, :] = all_ref[response, 0:64, :]
        out_ref[g, 64:128, :] = all_ref[excite, 0:64, :]


def split3(x):
    first = x.astype(BF)
    rest = x - first.astype(F32)
    second = rest.astype(BF)
    third = (rest - second.astype(F32)).astype(BF)
    return first.astype(F32), second.astype(F32), third.astype(F32)


def fan_kernel(mine_ref, omega_ref, damping_ref, out_ref):
    pieces = split3(omega_ref[...]) + split3(damping_ref[...])
    rows = lax.broadcasted_iota(jnp.int32, (16, 128), 0)
    table = jnp.zeros((16, 128), F32)
    for n, piece in enumerate(pieces):
        table = jnp.where(rows == n, piece, table)
    table = table.astype(BF)
    for y in range(4):
        for i in range(16):
            out_ref[y, 32 * i : 32 * i + 32, :] = mine_ref[i, 64:96, :]
            out_ref[y, 512 + 32 * i : 544 + 32 * i, :] = mine_ref[i, 96:128, :]
        for q in range(4):
            out_ref[y, 1024 + 32 * q : 1056 + 32 * q, :] = mine_ref[4 * y + q, 0:32, :]
            out_ref[y, 1152 + 32 * q : 1184 + 32 * q, :] = mine_ref[4 * y + q, 32:64, :]
        out_ref[y, 1280:1296, :] = table


def product_kernel(parts_ref, speeds_ref, out_ref):
    left = []
    weights = []
    for y in range(4):
        res_re = parts_ref[y, 1024:1152, :]
        res_im = parts_ref[y, 1152:1280, :]
        left.append(jnp.concatenate([res_re, res_im], axis=0))
        left.append(jnp.concatenate([-res_im, res_re], axis=0))
        table = parts_ref[y, 1280:1296, :].astype(F32)
        omega = table[0:1] + table[1:2] + table[2:3]
        damping = table[3:4] + table[4:5] + table[5:6]
        weights.append((omega, damping))
    left = jnp.concatenate(left, axis=1)
    for s in range(4):
        speed = speeds_ref[s]
        right = []
        for y in range(4):
            omega, damping = weights[y]
            a = omega * omega - speed * speed
            b = 2.0 * damping * omega * speed
            denom = a * a + b * b
            wre = a / denom
            wim = -b / denom
            ere = parts_ref[y, 0:512, :].astype(F32)
            eim = parts_ref[y, 512:1024, :].astype(F32)
            right.append((wre * ere - wim * eim).astype(BF))
            right.append((wre * eim + wim * ere).astype(BF))
        right = jnp.concatenate(right, axis=1)
        both = lax.dot_general(
            left, right, (((1,), (1,)), ((), ())), preferred_element_type=F32
        )
        for c in range(2):
            at = (2 * s + c) * 512
            out_ref[:, at : at + 512] = both[128 * c : 128 * c + 128].astype(BF)


def sum_kernel(parts_ref, out_ref):
    for s in range(4):
        for c in range(2):
            at = (2 * s + c) * 512
            total = parts_ref[0, :, at : at + 512].astype(F32)
            for x in range(1, 4):
                total = total + parts_ref[x, :, at : at + 512].astype(F32)
            out_ref[:, 0, s, c, :] = total


def shards(shapes, pairs, omega, damping, speeds):
    along_y = [[4 * y + x for y in range(4)] for x in range(4)]
    along_x = [[4 * y + x for x in range(4)] for y in range(4)]
    sliced = call(
        slice_kernel, jax.ShapeDtypeStruct((16, 80, 128), BF), [VMEM, SMEM], "slice_rows"
    )(shapes, pairs)
    regions = lax.all_to_all(sliced, "group", 0, 0, tiled=True)
    picked = call(
        pick_kernel, jax.ShapeDtypeStruct((16, 128, 128), BF), [VMEM], "pick_regions"
    )(regions)
    mine = lax.all_to_all(picked, "group", 0, 0, tiled=True)
    fanned = call(
        fan_kernel, jax.ShapeDtypeStruct((4, 1296, 128), BF), [VMEM] * 3, "fan_out"
    )(mine, omega.reshape(1, 128), damping.reshape(1, 128))
    parts = lax.all_to_all(fanned, "mode", 0, 0, tiled=True, axis_index_groups=along_y)
    partial = call(
        product_kernel, jax.ShapeDtypeStruct((128, 4096), BF), [VMEM, SMEM], "products"
    )(parts, speeds)
    terms = lax.all_to_all(
        partial.reshape(4, 32, 4096), "mode", 0, 0, tiled=True, axis_index_groups=along_x
    )
    return call(
        sum_kernel, jax.ShapeDtypeStruct((32, 1, 4, 2, 512), F32), [VMEM], "sum_terms"
    )(terms)


def solution(mesh):
    in_specs = (P(None, "group", None, "mode"), P("group", None), P("mode"), P("mode"), P())
    out_specs = P("mode", "group", None, None, None)
    return jax.shard_map(shards, mesh=mesh, in_specs=in_specs, out_specs=out_specs, check_vma=False)
```

```python
import functools

import jax
import jax.numpy as jnp
from jax import lax
from jax.experimental import pallas as pl
from jax.experimental.pallas import tpu as pltpu
from jax.sharding import PartitionSpec as P

BF = jnp.bfloat16
F32 = jnp.float32
VMEM = pl.BlockSpec(memory_space=pltpu.VMEM)
SMEM = pl.BlockSpec(memory_space=pltpu.SMEM)
PARAMS = pltpu.CompilerParams(vmem_limit_bytes=40 * 1024 * 1024)
ORDER = (2, 1, 3)
BLOCKS = 49


def call(kernel, out_shape, in_specs, name, flops=0, size=1 << 20):
    many = isinstance(out_shape, tuple)
    return pl.pallas_call(
        kernel,
        out_shape=out_shape,
        in_specs=in_specs,
        out_specs=tuple(VMEM for _ in out_shape) if many else VMEM,
        compiler_params=PARAMS,
        cost_estimate=pl.CostEstimate(flops=flops, bytes_accessed=size, transcendentals=0),
        name=name,
    )


def slice_kernel(shapes_ref, pairs_ref, out_ref):
    rows = lax.broadcasted_iota(jnp.int32, (16, 128), 0)
    pair = jnp.where(rows < 8, pairs_ref[0, 0], pairs_ref[0, 1])
    pair = pair.astype(F32).astype(BF)
    for i in range(16):
        out_ref[i, 0:32, :] = shapes_ref[0, 0, 32 * i : 32 * i + 32, :]
        out_ref[i, 32:64, :] = shapes_ref[1, 0, 32 * i : 32 * i + 32, :]
        out_ref[i, 64:80, :] = pair


def pick_kernel(all_ref, out_ref):
    for g in range(16):
        pair = all_ref[g, 64:80, :].astype(F32)
        response = pair[0, 0].astype(jnp.int32)
        excite = pair[8, 0].astype(jnp.int32)
        out_ref[g, 0:64, :] = all_ref[response, 0:64, :]
        out_ref[g, 64:128, :] = all_ref[excite, 0:64, :]


def split3(x):
    first = x.astype(BF)
    rest = x - first.astype(F32)
    second = rest.astype(BF)
    third = (rest - second.astype(F32)).astype(BF)
    return first.astype(F32), second.astype(F32), third.astype(F32)


def position():
    me = lax.axis_index("mode")
    return lax.div(me, 4), lax.rem(me, 4)


def response_slice(half, tile, part):
    return 4 * tile + part if half == 0 else 4 * part + tile


def fan_kernel(mine_ref, omega_ref, damping_ref, *out_refs):
    here = position()
    pieces = split3(omega_ref[...]) + split3(damping_ref[...])
    rows = lax.broadcasted_iota(jnp.int32, (16, 128), 0)
    table = jnp.zeros((16, 128), F32)
    for n, piece in enumerate(pieces):
        table = jnp.where(rows == n, piece, table)
    table = table.astype(BF)
    for half in range(2):
        for n, d in enumerate(ORDER):
            out_ref = out_refs[3 * half + n]
            tile = lax.rem(here[half] + d, 4)
            for i in range(8):
                for b in range(4):
                    out_ref[4 * i + b] = mine_ref[8 * half + i, 64 + 16 * b : 80 + 16 * b, :]
            for q in range(4):
                row_slice = response_slice(half, tile, q)
                for b in range(4):
                    out_ref[32 + 4 * q + b] = mine_ref[row_slice, 16 * b : 16 * b + 16, :]
            out_ref[48] = table


def product_kernel(half, mine_ref, omega_ref, damping_ref, one_ref, two_ref, three_ref, speeds_ref, *out_refs):
    here = position()
    tile, part = here[half], here[1 - half]
    left, excite, weights = [], [], []
    for ref in (mine_ref, one_ref, two_ref, three_ref):
        res_re, res_im = [], []
        for d in range(4):
            q = lax.rem(part + d, 4)
            if ref is mine_ref:
                row_slice = response_slice(half, tile, q)
                res_re.append(mine_ref[row_slice, 0:32, :])
                res_im.append(mine_ref[row_slice, 32:64, :])
            else:
                res_re.append(ref[pl.ds(32 + 4 * q, 2)].reshape(32, 128))
                res_im.append(ref[pl.ds(34 + 4 * q, 2)].reshape(32, 128))
        res_re = jnp.concatenate(res_re, axis=0)
        res_im = jnp.concatenate(res_im, axis=0)
        left.append(jnp.concatenate([res_re, res_im], axis=0))
        left.append(jnp.concatenate([-res_im, res_re], axis=0))
        if ref is mine_ref:
            ere = [mine_ref[8 * half + i, 64:96, :] for i in range(8)]
            eim = [mine_ref[8 * half + i, 96:128, :] for i in range(8)]
            weights.append((omega_ref[...], damping_ref[...]))
        else:
            ere = [ref[4 * i : 4 * i + 2].reshape(32, 128) for i in range(8)]
            eim = [ref[4 * i + 2 : 4 * i + 4].reshape(32, 128) for i in range(8)]
            table = ref[48].astype(F32)
            weights.append((table[0:1] + table[1:2] + table[2:3], table[3:4] + table[4:5] + table[5:6]))
        excite.append((jnp.concatenate(ere, axis=0), jnp.concatenate(eim, axis=0)))
    left = jnp.concatenate(left, axis=1)
    for s in range(4):
        speed = speeds_ref[s]
        right = []
        for (ere, eim), (omega, damping) in zip(excite, weights):
            ere, eim = ere.astype(F32), eim.astype(F32)
            a = omega * omega - speed * speed
            b = 2.0 * damping * omega * speed
            denom = a * a + b * b
            wre = a / denom
            wim = -b / denom
            right.append((wre * ere - wim * eim).astype(BF))
            right.append((wre * eim + wim * ere).astype(BF))
        right = jnp.concatenate(right, axis=1)
        both = lax.dot_general(
            left, right, (((1,), (1,)), ((), ())), preferred_element_type=F32
        )
        for c in range(2):
            at = (2 * s + c) * 256
            for d in range(4):
                row = 128 * c + 32 * d
                out_refs[d][:, at : at + 256] = both[row : row + 32].astype(BF)


def sum_kernel(*refs):
    out_ref = refs[-1]
    for half in range(2):
        for s in range(4):
            for c in range(2):
                at = (2 * s + c) * 256
                total = refs[4 * half][:, at : at + 256].astype(F32)
                for n in range(1, 4):
                    total = total + refs[4 * half + n][:, at : at + 256].astype(F32)
                out_ref[:, 0, s, c, 256 * half : 256 * half + 256] = total


def shift(value, axis, d):
    if axis == 0:
        perm = [(4 * y + x, 4 * ((y + d) % 4) + x) for y in range(4) for x in range(4)]
    else:
        perm = [(4 * y + x, 4 * y + (x + d) % 4) for y in range(4) for x in range(4)]
    return lax.ppermute(value, "mode", perm)


def shards(shapes, pairs, omega, damping, speeds):
    sliced = call(
        slice_kernel, jax.ShapeDtypeStruct((16, 80, 128), BF), [VMEM, SMEM], "slice_rows"
    )(shapes, pairs)
    regions = lax.all_to_all(sliced, "group", 0, 0, tiled=True)
    picked = call(
        pick_kernel, jax.ShapeDtypeStruct((16, 128, 128), BF), [VMEM], "pick_regions"
    )(regions)
    mine = lax.all_to_all(picked, "group", 0, 0, tiled=True)
    omega, damping = omega.reshape(1, 128), damping.reshape(1, 128)
    message = jax.ShapeDtypeStruct((BLOCKS, 16, 128), BF)
    fanned = call(fan_kernel, (message,) * 6, [VMEM] * 3, "fan_out")(mine, omega, damping)
    got = [[shift(fanned[3 * half + n], half, d) for n, d in enumerate(ORDER)] for half in range(2)]
    terms = []
    for half in range(2):
        block = jax.ShapeDtypeStruct((32, 2048), BF)
        made = call(
            functools.partial(product_kernel, half),
            (block,) * 4,
            [VMEM] * 6 + [SMEM],
            "products_%d" % half,
            flops=2 * 256 * 1024 * 1024,
        )(mine, omega, damping, *got[half], speeds)
        terms += [made[0]] + [shift(made[d], 1 - half, d) for d in ORDER]
    return call(
        sum_kernel, jax.ShapeDtypeStruct((32, 1, 4, 2, 512), F32), [VMEM] * 8, "sum_terms"
    )(*terms)


def solution(mesh):
    in_specs = (P(None, "group", None, "mode"), P("group", None), P("mode"), P("mode"), P())
    out_specs = P("mode", "group", None, None, None)
    return jax.shard_map(shards, mesh=mesh, in_specs=in_specs, out_specs=out_specs, check_vma=False)
```

```python
import jax
import jax.numpy as jnp
from jax import lax
from jax.experimental import pallas as pl
from jax.experimental.pallas import tpu as pltpu
from jax.sharding import PartitionSpec as P

BF = jnp.bfloat16
F32 = jnp.float32
VMEM = pl.BlockSpec(memory_space=pltpu.VMEM)
SMEM = pl.BlockSpec(memory_space=pltpu.SMEM)
PARAMS = pltpu.CompilerParams(vmem_limit_bytes=40 * 1024 * 1024)
EXCITE, RESPONSE, TABLE, ROWS = 0, 1024, 1280, 1296


def call(kernel, out_shape, in_specs, name, flops=0, size=1 << 20):
    many = isinstance(out_shape, tuple)
    return pl.pallas_call(
        kernel,
        out_shape=out_shape,
        in_specs=in_specs,
        out_specs=tuple(VMEM for _ in out_shape) if many else VMEM,
        compiler_params=PARAMS,
        cost_estimate=pl.CostEstimate(flops=flops, bytes_accessed=size, transcendentals=0),
        name=name,
    )


def partner(at, shifted):
    odd = at % 2
    return (at + 1 - 2 * (odd ^ shifted)) % 4


def peer(y, x, d, shifted):
    return (partner(y, shifted) if d & 2 else y), (partner(x, shifted) if d & 1 else x)


def slice_kernel(shapes_ref, pairs_ref, out_ref):
    rows = lax.broadcasted_iota(jnp.int32, (16, 128), 0)
    pair = jnp.where(rows < 8, pairs_ref[0, 0], pairs_ref[0, 1])
    pair = pair.astype(F32).astype(BF)
    for i in range(16):
        out_ref[i, 0:32, :] = shapes_ref[0, 0, 32 * i : 32 * i + 32, :]
        out_ref[i, 32:64, :] = shapes_ref[1, 0, 32 * i : 32 * i + 32, :]
        out_ref[i, 64:80, :] = pair


def pick_kernel(all_ref, out_ref):
    for g in range(16):
        pair = all_ref[g, 64:80, :].astype(F32)
        response = pair[0, 0].astype(jnp.int32)
        excite = pair[8, 0].astype(jnp.int32)
        out_ref[g, 0:64, :] = all_ref[response, 0:64, :]
        out_ref[g, 64:128, :] = all_ref[excite, 0:64, :]


def split3(x):
    first = x.astype(BF)
    rest = x - first.astype(F32)
    second = rest.astype(BF)
    third = (rest - second.astype(F32)).astype(BF)
    return first.astype(F32), second.astype(F32), third.astype(F32)


def fan_kernel(mine_ref, omega_ref, damping_ref, *out_refs):
    me = lax.axis_index("mode")
    core = lax.axis_index("group") % 2
    pieces = split3(omega_ref[...]) + split3(damping_ref[...])
    rows = lax.broadcasted_iota(jnp.int32, (16, 128), 0)
    table = jnp.zeros((16, 128), F32)
    for n, piece in enumerate(pieces):
        table = jnp.where(rows == n, piece, table)
    table = table.astype(BF)
    for d, out_ref in enumerate(out_refs):
        y, x = peer(me // 4, me % 4, d, core)
        for i in range(16):
            at = EXCITE + 32 * i
            out_ref[at : at + 32, :] = mine_ref[i, 64:96, :]
            out_ref[at + 512 : at + 544, :] = mine_ref[i, 96:128, :]
        for e in range(4):
            owner_y, owner_x = peer(y, x, e, 1 - core)
            owner = 4 * owner_y + owner_x
            at = RESPONSE + 32 * e
            out_ref[at : at + 32, :] = mine_ref[owner, 0:32, :]
            out_ref[at + 128 : at + 160, :] = mine_ref[owner, 32:64, :]
        out_ref[TABLE:ROWS, :] = table


def product_kernel(*refs):
    parts, speeds_ref, out_refs = refs[:4], refs[4], refs[5:]
    left, excite, weights = [], [], []
    for ref in parts:
        res_re = ref[RESPONSE : RESPONSE + 128, :]
        res_im = ref[RESPONSE + 128 : RESPONSE + 256, :]
        left.append(jnp.concatenate([res_re, res_im], axis=0))
        left.append(jnp.concatenate([-res_im, res_re], axis=0))
        table = ref[TABLE:ROWS, :].astype(F32)
        weights.append((table[0:1] + table[1:2] + table[2:3], table[3:4] + table[4:5] + table[5:6]))
    left = jnp.concatenate(left, axis=1)
    for s in range(4):
        speed = speeds_ref[s]
        right = []
        for ref, (omega, damping) in zip(parts, weights):
            ere = ref[EXCITE : EXCITE + 512, :].astype(F32)
            eim = ref[EXCITE + 512 : EXCITE + 1024, :].astype(F32)
            a = omega * omega - speed * speed
            b = 2.0 * damping * omega * speed
            denom = a * a + b * b
            wre = a / denom
            wim = -b / denom
            right.append((wre * ere - wim * eim).astype(BF))
            right.append((wre * eim + wim * ere).astype(BF))
        right = jnp.concatenate(right, axis=1)
        both = lax.dot_general(
            left, right, (((1,), (1,)), ((), ())), preferred_element_type=F32
        )
        for c in range(2):
            at = (2 * s + c) * 512
            for e in range(4):
                row = 128 * c + 32 * e
                out_refs[e][:, at : at + 512] = both[row : row + 32].astype(BF)


def sum_kernel(*refs):
    terms, out_ref = refs[:4], refs[4]
    for s in range(4):
        for c in range(2):
            at = (2 * s + c) * 512
            total = terms[0][:, at : at + 512].astype(F32)
            for ref in terms[1:]:
                total = total + ref[:, at : at + 512].astype(F32)
            out_ref[:, 0, s, c, :] = total


def exchange(value, d, flip):
    perm = []
    for g in range(16):
        for m in range(16):
            y, x = peer(m // 4, m % 4, d, (g % 2) ^ flip)
            perm.append((16 * g + m, 16 * g + 4 * y + x))
    return lax.ppermute(value, ("group", "mode"), perm)


def shards(shapes, pairs, omega, damping, speeds):
    sliced = call(
        slice_kernel, jax.ShapeDtypeStruct((16, 80, 128), BF), [VMEM, SMEM], "slice_rows"
    )(shapes, pairs)
    regions = lax.all_to_all(sliced, "group", 0, 0, tiled=True)
    picked = call(
        pick_kernel, jax.ShapeDtypeStruct((16, 128, 128), BF), [VMEM], "pick_regions"
    )(regions)
    mine = lax.all_to_all(picked, "group", 0, 0, tiled=True)
    omega, damping = omega.reshape(1, 128), damping.reshape(1, 128)
    message = jax.ShapeDtypeStruct((ROWS, 128), BF)
    fanned = call(fan_kernel, (message,) * 4, [VMEM] * 3, "fan_out")(mine, omega, damping)
    parts = [fanned[0]] + [exchange(fanned[d], d, 0) for d in (3, 1, 2)]
    block = jax.ShapeDtypeStruct((32, 4096), BF)
    made = call(
        product_kernel, (block,) * 4, [VMEM] * 4 + [SMEM], "products", flops=1 << 30
    )(*parts, speeds)
    terms = [made[0]] + [exchange(made[e], e, 1) for e in (3, 1, 2)]
    return call(
        sum_kernel, jax.ShapeDtypeStruct((32, 1, 4, 2, 512), F32), [VMEM] * 4, "sum_terms"
    )(*terms)


def solution(mesh):
    in_specs = (P(None, "group", None, "mode"), P("group", None), P("mode"), P("mode"), P())
    out_specs = P("mode", "group", None, None, None)
    return jax.shard_map(shards, mesh=mesh, in_specs=in_specs, out_specs=out_specs, check_vma=False)
```

```python
import jax
import jax.numpy as jnp
from jax import lax
from jax.experimental import pallas as pl
from jax.experimental.pallas import tpu as pltpu
from jax.sharding import PartitionSpec as P

BF = jnp.bfloat16
F32 = jnp.float32
VMEM = pl.BlockSpec(memory_space=pltpu.VMEM)
SMEM = pl.BlockSpec(memory_space=pltpu.SMEM)
HBM = pl.BlockSpec(memory_space=pltpu.HBM)
PARAMS = pltpu.CompilerParams(vmem_limit_bytes=40 * 1024 * 1024)
EXCITE, RESPONSE, TABLE, ROWS = 0, 1024, 1280, 1296


def call(kernel, out_shape, in_specs, name, flops=0, size=1 << 20, scratch=(), aliases=None, params=PARAMS, out_spec=VMEM):
    many = isinstance(out_shape, tuple)
    return pl.pallas_call(
        kernel,
        out_shape=out_shape,
        in_specs=in_specs,
        out_specs=tuple(out_spec for _ in out_shape) if many else out_spec,
        scratch_shapes=list(scratch),
        input_output_aliases=aliases or {},
        compiler_params=params,
        cost_estimate=pl.CostEstimate(flops=flops, bytes_accessed=size, transcendentals=0),
        name=name,
    )


def partner(at, shifted):
    odd = at % 2
    return (at + 1 - 2 * (odd ^ shifted)) % 4


def peer(y, x, d, shifted):
    return (partner(y, shifted) if d & 2 else y), (partner(x, shifted) if d & 1 else x)


def locate(region, me):
    core = me % 2
    below = (me // 2 - region // 2) % 8
    steps = jnp.where(core == 0, below, (8 - below) % 8)
    same = region % 2 == core
    slot = jnp.where(same, steps, jnp.where(steps == 0, 8, 4 + steps))
    return jnp.where(slot < 8, jnp.where(steps > 4, 8, slot), 8)


def prepare_kernel(shapes_ref, omega_ref, damping_ref, own_ref, table_ref):
    own_ref[...] = shapes_ref[:, 0]
    pieces = split3(omega_ref[...]) + split3(damping_ref[...])
    rows = lax.broadcasted_iota(jnp.int32, (16, 128), 0)
    table = jnp.zeros((16, 128), F32)
    for n, piece in enumerate(pieces):
        table = jnp.where(rows == n, piece, table)
    table_ref[...] = table.astype(BF)


def pick_kernel(pair_ref, *refs):
    regions, out_ref = refs[:8], refs[8]
    me = lax.axis_index("group")
    for n in range(2):
        slot = locate(pair_ref[0, n], me)
        for k, ref in enumerate(regions):

            @pl.when(slot == k)
            def _(ref=ref):
                out_ref[n] = ref[...]


def split3(x):
    first = x.astype(BF)
    rest = x - first.astype(F32)
    second = rest.astype(BF)
    third = (rest - second.astype(F32)).astype(BF)
    return first.astype(F32), second.astype(F32), third.astype(F32)


def fan_kernel(pair_ref, table_ref, *refs):
    regions, other_ref, out_refs, picked_ref = refs[:8], refs[8], refs[9:13], refs[13]
    me = lax.axis_index("group")
    for n in range(2):
        slot = locate(pair_ref[0, n], me)
        for k, ref in enumerate(regions):

            @pl.when(slot == k)
            def _(ref=ref):
                picked_ref[n] = ref[...]

        @pl.when(slot == 8)
        def _():
            picked_ref[n] = other_ref[n]

    core = me % 2
    at_mode = lax.axis_index("mode")
    for d, out_ref in enumerate(out_refs):
        y, x = peer(at_mode // 4, at_mode % 4, d, core)
        out_ref[EXCITE : EXCITE + 512, :] = picked_ref[1, 0]
        out_ref[EXCITE + 512 : EXCITE + 1024, :] = picked_ref[1, 1]
        for e in range(4):
            owner_y, owner_x = peer(y, x, e, 1 - core)
            owned = pl.ds(pl.multiple_of(32 * (4 * owner_y + owner_x), 32), 32)
            at = RESPONSE + 32 * e
            out_ref[at : at + 32, :] = picked_ref[0, 0, owned, :]
            out_ref[at + 128 : at + 160, :] = picked_ref[0, 1, owned, :]
        out_ref[TABLE:ROWS, :] = table_ref[...]


def share(parts, speeds_ref):
    left, modes = [], []
    for ref in parts:
        res_re = ref[RESPONSE : RESPONSE + 128, :]
        res_im = ref[RESPONSE + 128 : RESPONSE + 256, :]
        left.append(jnp.concatenate([res_re, res_im], axis=0))
        left.append(jnp.concatenate([-res_im, res_re], axis=0))
        table = ref[TABLE:ROWS, :].astype(F32)
        modes.append((table[0:1] + table[1:2] + table[2:3], table[3:4] + table[4:5] + table[5:6]))
    left = jnp.concatenate(left, axis=1)
    for s in range(4):
        speed = speeds_ref[s]
        right = []
        for ref, (omega, damping) in zip(parts, modes):
            ere = ref[EXCITE : EXCITE + 512, :].astype(F32)
            eim = ref[EXCITE + 512 : EXCITE + 1024, :].astype(F32)
            a = omega * omega - speed * speed
            b = 2.0 * damping * omega * speed
            denom = a * a + b * b
            wre = a / denom
            wim = -b / denom
            right.append((wre * ere - wim * eim).astype(BF))
            right.append((wre * eim + wim * ere).astype(BF))
        right = jnp.concatenate(right, axis=1)
        yield s, lax.dot_general(
            left, right, (((1,), (1,)), ((), ())), preferred_element_type=F32
        )


def first_kernel(part_ref, speeds_ref, out_ref):
    for s, both in share([part_ref], speeds_ref):
        out_ref[s] = both


def next_kernel(total_ref, part_ref, speeds_ref, out_ref):
    for s, both in share([part_ref], speeds_ref):
        out_ref[s] = total_ref[s] + both


def last_kernel(total_ref, part_ref, other_ref, speeds_ref, own_ref, *out_refs):
    for s, both in share([part_ref, other_ref], speeds_ref):
        both = total_ref[s] + both
        for c in range(2):
            at = (2 * s + c) * 512
            own_ref[:, at : at + 512] = both[128 * c : 128 * c + 32]
            for e in range(1, 4):
                row = 128 * c + 32 * e
                out_refs[e - 1][:, at : at + 512] = both[row : row + 32].astype(BF)


def sum_kernel(*refs):
    terms, out_ref = refs[:4], refs[4]
    for s in range(4):
        for c in range(2):
            at = (2 * s + c) * 512
            total = terms[0][:, at : at + 512]
            for ref in terms[1:]:
                total = total + ref[:, at : at + 512].astype(F32)
            out_ref[:, 0, s, c, :] = total


def exchange(value, d, flip):
    perm = []
    for g in range(16):
        for m in range(16):
            y, x = peer(m // 4, m % 4, d, (g % 2) ^ flip)
            perm.append((16 * g + m, 16 * g + 4 * y + x))
    return lax.ppermute(value, ("group", "mode"), perm)


def along_z(value, crossing=False):
    perm = []
    for g in range(16):
        core = g % 2 ^ crossing
        perm.append((g, 2 * ((g // 2 + 1 - 2 * core) % 8) + core))
    return lax.ppermute(value, "group", perm)


def swap_cores(value):
    return lax.ppermute(value, "group", [(g, g ^ 1) for g in range(16)])


def shards(shapes, pairs, omega, damping, speeds):
    a1 = along_z(shapes.reshape(2, 512, 128))
    own, table = call(
        prepare_kernel,
        (jax.ShapeDtypeStruct((2, 512, 128), BF), jax.ShapeDtypeStruct((16, 128), BF)),
        [VMEM] * 3,
        "prepare",
    )(shapes, omega.reshape(1, 128), damping.reshape(1, 128))
    b1 = along_z(own, crossing=True)
    a1, other_pair = lax.optimization_barrier((a1, swap_cores(pairs)))
    a2 = along_z(a1)
    b2 = along_z(b1)
    a3 = along_z(a2)
    b3 = along_z(b2)
    a4 = along_z(a3)
    regions = (own, a1, a2, a3, a4, b1, b2, b3)
    other = jax.ShapeDtypeStruct((2, 2, 512, 128), BF)
    wanted = call(pick_kernel, other, [SMEM] + [VMEM] * 8, "pick_regions")(other_pair, *regions)
    message = jax.ShapeDtypeStruct((ROWS, 128), BF)
    fanned = call(
        fan_kernel,
        (message,) * 4,
        [SMEM] + [VMEM] * 10,
        "fan_out",
        scratch=[pltpu.VMEM((2, 2, 512, 128), BF)],
    )(pairs, table, *regions, swap_cores(wanted))
    parts = [fanned[0]] + [exchange(fanned[d], d, 0) for d in (3, 1, 2)]
    sums = jax.ShapeDtypeStruct((4, 256, 512), F32)
    total = call(first_kernel, sums, [VMEM, SMEM], "product_0", flops=1 << 28)(parts[0], speeds)
    total = call(
        next_kernel, sums, [VMEM, VMEM, SMEM], "product_1", flops=1 << 28, aliases={0: 0}
    )(total, parts[1], speeds)
    block = jax.ShapeDtypeStruct((32, 4096), BF)
    made = call(
        last_kernel,
        (jax.ShapeDtypeStruct((32, 4096), F32), block, block, block),
        [VMEM, VMEM, VMEM, SMEM],
        "product_2",
        flops=1 << 29,
    )(total, parts[2], parts[3], speeds)
    terms = [made[0]] + [exchange(made[e], e, 1) for e in (3, 1, 2)]
    return call(
        sum_kernel, jax.ShapeDtypeStruct((32, 1, 4, 2, 512), F32), [VMEM] * 4, "sum_terms"
    )(*terms)


def solution(mesh):
    in_specs = (P(None, "group", None, "mode"), P("group", None), P("mode"), P("mode"), P())
    out_specs = P("mode", "group", None, None, None)
    return jax.shard_map(shards, mesh=mesh, in_specs=in_specs, out_specs=out_specs, check_vma=False)
```

```python
import jax
import jax.numpy as jnp
from jax import lax
from jax.experimental import pallas as pl
from jax.experimental.pallas import tpu as pltpu
from jax.sharding import PartitionSpec as P

BF = jnp.bfloat16
F32 = jnp.float32
VMEM = pl.BlockSpec(memory_space=pltpu.VMEM)
SMEM = pl.BlockSpec(memory_space=pltpu.SMEM)
HBM = pl.BlockSpec(memory_space=pltpu.HBM)
PARAMS = pltpu.CompilerParams(vmem_limit_bytes=40 * 1024 * 1024)
EXCITE, RESPONSE, TABLE, ROWS = 0, 1024, 1280, 1296


def call(kernel, out_shape, in_specs, name, flops=0, size=1 << 20, scratch=(), aliases=None, params=PARAMS, out_spec=VMEM):
    many = isinstance(out_shape, tuple)
    return pl.pallas_call(
        kernel,
        out_shape=out_shape,
        in_specs=in_specs,
        out_specs=tuple(out_spec for _ in out_shape) if many else out_spec,
        scratch_shapes=list(scratch),
        input_output_aliases=aliases or {},
        compiler_params=params,
        cost_estimate=pl.CostEstimate(flops=flops, bytes_accessed=size, transcendentals=0),
        name=name,
    )


def partner(at, shifted):
    odd = at % 2
    return (at + 1 - 2 * (odd ^ shifted)) % 4


def peer(y, x, d, shifted):
    return (partner(y, shifted) if d & 2 else y), (partner(x, shifted) if d & 1 else x)


def locate(region, me):
    core = me % 2
    below = (me // 2 - region // 2) % 8
    steps = jnp.where(core == 0, below, (8 - below) % 8)
    same = region % 2 == core
    near = jnp.where(same, steps, jnp.where(steps == 0, 8, 3 + steps))
    far = jnp.where(steps > 4, 8, jnp.where(same, 7, 9))
    return jnp.where(steps < 4, near, far)


def pick_kernel(pair_ref, *refs):
    regions, out_ref = refs[:7], refs[7]
    me = lax.axis_index("group")
    pair = pair_ref[...]
    for n in range(2):
        slot = locate(pair[0, n], me)
        for k, ref in enumerate(regions):

            @pl.when(slot == k)
            def _(ref=ref):
                out_ref[n] = ref[...]


def split3(x):
    first = x.astype(BF)
    rest = x - first.astype(F32)
    second = rest.astype(BF)
    third = (rest - second.astype(F32)).astype(BF)
    return first.astype(F32), second.astype(F32), third.astype(F32)


def prepare_kernel(shapes_ref, omega_ref, damping_ref, speeds_ref, own_ref, table_ref, speed_rows_ref):
    own_ref[...] = shapes_ref[:, 0]
    pieces = split3(omega_ref[...]) + split3(damping_ref[...])
    rows = lax.broadcasted_iota(jnp.int32, (16, 128), 0)
    table = jnp.zeros((16, 128), F32)
    for n, piece in enumerate(pieces):
        table = jnp.where(rows == n, piece, table)
    table_ref[...] = table.astype(BF)
    rows = lax.broadcasted_iota(jnp.int32, (8, 128), 0)
    speeds = jnp.zeros((8, 128), F32)
    for s in range(4):
        speeds = jnp.where(rows == s, speeds_ref[s], speeds)
    speed_rows_ref[...] = speeds


def fan_kernel(pair_ref, table_ref, *refs):
    regions, other_ref, far_ref, out_refs, picked_ref = refs[:8], refs[8], refs[9], refs[10:14], refs[14]
    me = lax.axis_index("group")
    pair = pair_ref[...]
    for n in range(2):
        slot = locate(pair[0, n], me)
        for k, ref in enumerate(regions + (other_ref.at[n], far_ref)):

            @pl.when(slot == k)
            def _(ref=ref):
                picked_ref[n] = ref[...]

    core = me % 2
    at_mode = lax.axis_index("mode")
    for d, out_ref in enumerate(out_refs):
        y, x = peer(at_mode // 4, at_mode % 4, d, core)
        out_ref[EXCITE : EXCITE + 512, :] = picked_ref[1, 0]
        out_ref[EXCITE + 512 : EXCITE + 1024, :] = picked_ref[1, 1]
        for e in range(4):
            owner_y, owner_x = peer(y, x, e, 1 - core)
            owned = pl.ds(pl.multiple_of(32 * (4 * owner_y + owner_x), 32), 32)
            at = RESPONSE + 32 * e
            out_ref[at : at + 32, :] = picked_ref[0, 0, owned, :]
            out_ref[at + 128 : at + 160, :] = picked_ref[0, 1, owned, :]
        out_ref[TABLE:ROWS, :] = table_ref[...]


def share(parts, speeds_ref):
    left, modes = [], []
    for ref in parts:
        res_re = ref[RESPONSE : RESPONSE + 128, :]
        res_im = ref[RESPONSE + 128 : RESPONSE + 256, :]
        left.append(jnp.concatenate([res_re, res_im], axis=0))
        left.append(jnp.concatenate([-res_im, res_re], axis=0))
        table = ref[TABLE:ROWS, :].astype(F32)
        modes.append((table[0:1] + table[1:2] + table[2:3], table[3:4] + table[4:5] + table[5:6]))
    left = jnp.concatenate(left, axis=1)
    for s in range(4):
        speed = speeds_ref[s : s + 1, :]
        right = []
        for ref, (omega, damping) in zip(parts, modes):
            ere = ref[EXCITE : EXCITE + 512, :].astype(F32)
            eim = ref[EXCITE + 512 : EXCITE + 1024, :].astype(F32)
            a = omega * omega - speed * speed
            b = 2.0 * damping * omega * speed
            denom = a * a + b * b
            wre = a / denom
            wim = -b / denom
            right.append((wre * ere - wim * eim).astype(BF))
            right.append((wre * eim + wim * ere).astype(BF))
        right = jnp.concatenate(right, axis=1)
        yield s, lax.dot_general(
            left, right, (((1,), (1,)), ((), ())), preferred_element_type=F32
        )


def first_kernel(part_ref, speeds_ref, out_ref):
    for s, both in share([part_ref], speeds_ref):
        out_ref[s] = both


def next_kernel(total_ref, part_ref, speeds_ref, out_ref):
    for s, both in share([part_ref], speeds_ref):
        out_ref[s] = total_ref[s] + both


def last_kernel(total_ref, part_ref, other_ref, speeds_ref, own_ref, *out_refs):
    for s, both in share([part_ref, other_ref], speeds_ref):
        both = total_ref[s] + both
        for c in range(2):
            at = (2 * s + c) * 512
            own_ref[:, at : at + 512] = both[128 * c : 128 * c + 32]
            for e in range(1, 4):
                row = 128 * c + 32 * e
                out_refs[e - 1][:, at : at + 512] = both[row : row + 32].astype(BF)


def sum_kernel(*refs):
    terms, out_ref = refs[:4], refs[4]
    for s in range(4):
        for c in range(2):
            at = (2 * s + c) * 512
            total = terms[0][:, at : at + 512]
            for ref in terms[1:]:
                total = total + ref[:, at : at + 512].astype(F32)
            out_ref[:, 0, s, c, :] = total


def exchange(value, d, flip):
    perm = []
    for g in range(16):
        for m in range(16):
            y, x = peer(m // 4, m % 4, d, (g % 2) ^ flip)
            perm.append((16 * g + m, 16 * g + 4 * y + x))
    return lax.ppermute(value, ("group", "mode"), perm)


def along_z(value, crossing=False):
    perm = []
    for g in range(16):
        core = g % 2 ^ crossing
        perm.append((g, 2 * ((g // 2 + 1 - 2 * core) % 8) + core))
    return lax.ppermute(value, "group", perm)


def swap_cores(value):
    return lax.ppermute(value, "group", [(g, g ^ 1) for g in range(16)])


def shards(shapes, pairs, omega, damping, speeds):
    a1 = along_z(shapes.reshape(2, 512, 128))
    own, table, speed_rows = call(
        prepare_kernel,
        (
            jax.ShapeDtypeStruct((2, 512, 128), BF),
            jax.ShapeDtypeStruct((16, 128), BF),
            jax.ShapeDtypeStruct((8, 128), F32),
        ),
        [VMEM] * 3 + [SMEM],
        "prepare",
    )(shapes, omega.reshape(1, 128), damping.reshape(1, 128), speeds)
    b1 = along_z(own, crossing=True)
    a1, other_pair = lax.optimization_barrier((a1, swap_cores(pairs)))
    a2 = along_z(a1)
    b2 = along_z(b1)
    a3 = along_z(a2)
    b3 = along_z(b2)
    a4 = along_z(a3)
    regions = (own, a1, a2, a3, b1, b2, b3)
    other = jax.ShapeDtypeStruct((2, 2, 512, 128), BF)
    wanted = call(pick_kernel, other, [VMEM] * 8, "pick_regions")(other_pair, *regions)
    message = jax.ShapeDtypeStruct((ROWS, 128), BF)
    fanned = call(
        fan_kernel,
        (message,) * 4,
        [VMEM] * 12,
        "fan_out",
        scratch=[pltpu.VMEM((2, 2, 512, 128), BF)],
    )(pairs, table, *regions, a4, swap_cores(wanted), swap_cores(a4))
    parts = [fanned[0]] + [exchange(fanned[d], d, 0) for d in (3, 1, 2)]
    sums = jax.ShapeDtypeStruct((4, 256, 512), F32)
    total = call(first_kernel, sums, [VMEM] * 2, "product_0", flops=1 << 28)(parts[0], speed_rows)
    total = call(
        next_kernel, sums, [VMEM] * 3, "product_1", flops=1 << 28, aliases={0: 0}
    )(total, parts[1], speed_rows)
    block = jax.ShapeDtypeStruct((32, 4096), BF)
    made = call(
        last_kernel,
        (jax.ShapeDtypeStruct((32, 4096), F32), block, block, block),
        [VMEM] * 4,
        "product_2",
        flops=1 << 29,
    )(total, parts[2], parts[3], speed_rows)
    terms = [made[0]] + [exchange(made[e], e, 1) for e in (3, 1, 2)]
    return call(
        sum_kernel, jax.ShapeDtypeStruct((32, 1, 4, 2, 512), F32), [VMEM] * 4, "sum_terms"
    )(*terms)


def solution(mesh):
    in_specs = (P(None, "group", None, "mode"), P("group", None), P("mode"), P("mode"), P())
    out_specs = P("mode", "group", None, None, None)
    return jax.shard_map(shards, mesh=mesh, in_specs=in_specs, out_specs=out_specs, check_vma=False)
```

```python
import jax
import jax.numpy as jnp
from jax import lax
from jax.experimental import pallas as pl
from jax.experimental.pallas import tpu as pltpu
from jax.sharding import PartitionSpec as P

BF = jnp.bfloat16
F32 = jnp.float32
VMEM = pl.BlockSpec(memory_space=pltpu.VMEM)
SMEM = pl.BlockSpec(memory_space=pltpu.SMEM)
HBM = pl.BlockSpec(memory_space=pltpu.HBM)
PARAMS = pltpu.CompilerParams(vmem_limit_bytes=40 * 1024 * 1024)
EXCITE, RESPONSE, TABLE, ROWS = 0, 1024, 1280, 1296


def call(kernel, out_shape, in_specs, name, flops=0, size=1 << 20, scratch=(), aliases=None, params=PARAMS, out_spec=VMEM):
    many = isinstance(out_shape, tuple)
    return pl.pallas_call(
        kernel,
        out_shape=out_shape,
        in_specs=in_specs,
        out_specs=tuple(out_spec for _ in out_shape) if many else out_spec,
        scratch_shapes=list(scratch),
        input_output_aliases=aliases or {},
        compiler_params=params,
        cost_estimate=pl.CostEstimate(flops=flops, bytes_accessed=size, transcendentals=0),
        name=name,
    )


def partner(at, shifted):
    odd = at % 2
    return (at + 1 - 2 * (odd ^ shifted)) % 4


def peer(y, x, d, shifted):
    return (partner(y, shifted) if d & 2 else y), (partner(x, shifted) if d & 1 else x)


A_UP = (0, 0, 0, 0, 1)
B_UP = (1, 0, 0, 1)


def step(value, k, up):
    perm = []
    for z in range(8):
        perm.append((2 * z + up[k - 1], 2 * ((z + 1) % 8) + up[k]))
        perm.append((2 * z + 1 - up[k - 1], 2 * ((z - 1) % 8) + 1 - up[k]))
    return lax.ppermute(value, "group", perm)


def locate(region, me):
    core, kind = me % 2, region % 2
    below = (me // 2 - region // 2) % 8
    slot = jnp.where(kind == core, 0, 8)
    for k in range(1, 5):
        for way, steps in ((0, below), (1, 8 - below)):
            on = A_UP[k] ^ way
            here = (steps == k) & (kind == way)
            slot = jnp.where(here, jnp.where(core == on, k if k < 4 else 7, 8 if k < 4 else 9), slot)
            if k < 4:
                on = B_UP[k] ^ way
                here = (steps == k) & (kind != way)
                slot = jnp.where(here, jnp.where(core == on, 3 + k, 8), slot)
    return slot


def pick_kernel(pair_ref, *refs):
    regions, out_ref = refs[:7], refs[7]
    me = lax.axis_index("group")
    pair = pair_ref[...]
    for n in range(2):
        slot = locate(pair[0, n], me)
        for k, ref in enumerate(regions):

            @pl.when(slot == k)
            def _(ref=ref):
                out_ref[n] = ref[...]


def split3(x):
    first = x.astype(BF)
    rest = x - first.astype(F32)
    second = rest.astype(BF)
    third = (rest - second.astype(F32)).astype(BF)
    return first.astype(F32), second.astype(F32), third.astype(F32)


def prepare_kernel(shapes_ref, omega_ref, damping_ref, speeds_ref, own_ref, table_ref, speed_rows_ref):
    own_ref[...] = shapes_ref[:, 0]
    pieces = split3(omega_ref[...]) + split3(damping_ref[...])
    rows = lax.broadcasted_iota(jnp.int32, (16, 128), 0)
    table = jnp.zeros((16, 128), F32)
    for n, piece in enumerate(pieces):
        table = jnp.where(rows == n, piece, table)
    table_ref[...] = table.astype(BF)
    rows = lax.broadcasted_iota(jnp.int32, (8, 128), 0)
    speeds = jnp.zeros((8, 128), F32)
    for s in range(4):
        speeds = jnp.where(rows == s, speeds_ref[s], speeds)
    speed_rows_ref[...] = speeds


def fan_kernel(pair_ref, table_ref, *refs):
    regions, other_ref, far_ref, out_refs, picked_ref = refs[:8], refs[8], refs[9], refs[10:14], refs[14]
    me = lax.axis_index("group")
    pair = pair_ref[...]
    for n in range(2):
        slot = locate(pair[0, n], me)
        for k, ref in enumerate(regions + (other_ref.at[n], far_ref)):

            @pl.when(slot == k)
            def _(ref=ref):
                picked_ref[n] = ref[...]

    core = me % 2
    at_mode = lax.axis_index("mode")
    for d, out_ref in enumerate(out_refs):
        y, x = peer(at_mode // 4, at_mode % 4, d, 1 - core)
        out_ref[EXCITE : EXCITE + 512, :] = picked_ref[1, 0]
        out_ref[EXCITE + 512 : EXCITE + 1024, :] = picked_ref[1, 1]
        for e in range(4):
            owner_y, owner_x = peer(y, x, e, core)
            owned = pl.ds(pl.multiple_of(32 * (4 * owner_y + owner_x), 32), 32)
            at = RESPONSE + 32 * e
            out_ref[at : at + 32, :] = picked_ref[0, 0, owned, :]
            out_ref[at + 128 : at + 160, :] = picked_ref[0, 1, owned, :]
        out_ref[TABLE:ROWS, :] = table_ref[...]


def weights(table, speed):
    omega = table[0:1] + table[1:2] + table[2:3]
    damping = table[3:4] + table[4:5] + table[5:6]
    a = omega * omega - speed * speed
    b = 2.0 * damping * omega * speed
    denom = a * a + b * b
    return a / denom, -b / denom


def share(parts, speeds_ref):
    left, modes = [], []
    for ref in parts:
        res_re = ref[RESPONSE : RESPONSE + 128, :]
        res_im = ref[RESPONSE + 128 : RESPONSE + 256, :]
        left.append(jnp.concatenate([res_re, res_im], axis=0))
        left.append(jnp.concatenate([-res_im, res_re], axis=0))
        modes.append(ref[TABLE:ROWS, :].astype(F32))
    left = jnp.concatenate(left, axis=1)
    for s in range(4):
        right = []
        for ref, table in zip(parts, modes):
            wre, wim = weights(table, speeds_ref[s : s + 1, :])
            ere = ref[EXCITE : EXCITE + 512, :].astype(F32)
            eim = ref[EXCITE + 512 : EXCITE + 1024, :].astype(F32)
            right.append((wre * ere - wim * eim).astype(BF))
            right.append((wre * eim + wim * ere).astype(BF))
        right = jnp.concatenate(right, axis=1)
        yield s, lax.dot_general(
            left, right, (((1,), (1,)), ((), ())), preferred_element_type=F32
        )


def first_kernel(part_ref, speeds_ref, out_ref):
    for s, both in share([part_ref], speeds_ref):
        out_ref[s] = both


def next_kernel(total_ref, part_ref, speeds_ref, out_ref):
    for s, both in share([part_ref], speeds_ref):
        out_ref[s] = total_ref[s] + both


def last_kernel(total_ref, part_ref, other_ref, speeds_ref, own_ref, *out_refs):
    parts = (part_ref, other_ref)
    right, modes = [], []
    for ref in parts:
        right.append(ref[EXCITE : EXCITE + 512, :])
        right.append(ref[EXCITE + 512 : EXCITE + 1024, :])
        modes.append(ref[TABLE:ROWS, :].astype(F32))
    right = jnp.concatenate(right, axis=1)
    for s in range(4):
        left = []
        for ref, table in zip(parts, modes):
            wre, wim = weights(table, speeds_ref[s : s + 1, :])
            rre = ref[RESPONSE : RESPONSE + 128, :].astype(F32)
            rim = ref[RESPONSE + 128 : RESPONSE + 256, :].astype(F32)
            lre = wre * rre - wim * rim
            lim = wre * rim + wim * rre
            left.append(jnp.concatenate([lre, lim], axis=0).astype(BF))
            left.append(jnp.concatenate([-lim, lre], axis=0).astype(BF))
        both = total_ref[s] + lax.dot_general(
            jnp.concatenate(left, axis=1),
            right,
            (((1,), (1,)), ((), ())),
            preferred_element_type=F32,
        )
        for c in range(2):
            at = (2 * s + c) * 512
            own_ref[:, at : at + 512] = both[128 * c : 128 * c + 32]
            for e in range(1, 4):
                row = 128 * c + 32 * e
                out_refs[e - 1][:, at : at + 512] = both[row : row + 32].astype(BF)


def sum_kernel(*refs):
    terms, out_ref = refs[:4], refs[4]
    for s in range(4):
        for c in range(2):
            at = (2 * s + c) * 512
            total = terms[0][:, at : at + 512]
            for ref in terms[1:]:
                total = total + ref[:, at : at + 512].astype(F32)
            out_ref[:, 0, s, c, :] = total


def exchange(value, d, flip):
    perm = []
    for g in range(16):
        for m in range(16):
            y, x = peer(m // 4, m % 4, d, 1 ^ (g % 2) ^ flip)
            perm.append((16 * g + m, 16 * g + 4 * y + x))
    return lax.ppermute(value, ("group", "mode"), perm)


def swap_cores(value):
    return lax.ppermute(value, "group", [(g, g ^ 1) for g in range(16)])


def shards(shapes, pairs, omega, damping, speeds):
    a1 = step(shapes.reshape(2, 512, 128), 1, A_UP)
    own, table, speed_rows = call(
        prepare_kernel,
        (
            jax.ShapeDtypeStruct((2, 512, 128), BF),
            jax.ShapeDtypeStruct((16, 128), BF),
            jax.ShapeDtypeStruct((8, 128), F32),
        ),
        [VMEM] * 3 + [SMEM],
        "prepare",
    )(shapes, omega.reshape(1, 128), damping.reshape(1, 128), speeds)
    b1 = step(own, 1, B_UP)
    a1, other_pair = lax.optimization_barrier((a1, swap_cores(pairs)))
    a2 = step(a1, 2, A_UP)
    b2 = step(b1, 2, B_UP)
    a3 = step(a2, 3, A_UP)
    b3 = step(b2, 3, B_UP)
    a4 = step(a3, 4, A_UP)
    regions = (own, a1, a2, a3, b1, b2, b3)
    other = jax.ShapeDtypeStruct((2, 2, 512, 128), BF)
    wanted = call(pick_kernel, other, [VMEM] * 8, "pick_regions")(other_pair, *regions)
    message = jax.ShapeDtypeStruct((ROWS, 128), BF)
    fanned = call(
        fan_kernel,
        (message,) * 4,
        [VMEM] * 12,
        "fan_out",
        scratch=[pltpu.VMEM((2, 2, 512, 128), BF)],
    )(pairs, table, *regions, a4, swap_cores(wanted), swap_cores(a4))
    parts = [fanned[0]] + [exchange(fanned[d], d, 0) for d in (3, 2, 1)]
    sums = jax.ShapeDtypeStruct((4, 256, 512), F32)
    total = call(first_kernel, sums, [VMEM] * 2, "product_0", flops=1 << 28)(parts[0], speed_rows)
    total = call(
        next_kernel, sums, [VMEM] * 3, "product_1", flops=1 << 28, aliases={0: 0}
    )(total, parts[1], speed_rows)
    block = jax.ShapeDtypeStruct((32, 4096), BF)
    made = call(
        last_kernel,
        (jax.ShapeDtypeStruct((32, 4096), F32), block, block, block),
        [VMEM] * 4,
        "product_2",
        flops=1 << 29,
    )(total, parts[2], parts[3], speed_rows)
    terms = [made[0]] + [exchange(made[e], e, 1) for e in (3, 2, 1)]
    return call(
        sum_kernel, jax.ShapeDtypeStruct((32, 1, 4, 2, 512), F32), [VMEM] * 4, "sum_terms"
    )(*terms)


def solution(mesh):
    in_specs = (P(None, "group", None, "mode"), P("group", None), P("mode"), P("mode"), P())
    out_specs = P("mode", "group", None, None, None)
    return jax.shard_map(shards, mesh=mesh, in_specs=in_specs, out_specs=out_specs, check_vma=False)
```

```python
import jax
import jax.numpy as jnp
from jax import lax
from jax.experimental import pallas as pl
from jax.experimental.pallas import tpu as pltpu
from jax.sharding import PartitionSpec as P

BF = jnp.bfloat16
F32 = jnp.float32
VMEM = pl.BlockSpec(memory_space=pltpu.VMEM)
SMEM = pl.BlockSpec(memory_space=pltpu.SMEM)
HBM = pl.BlockSpec(memory_space=pltpu.HBM)
PARAMS = pltpu.CompilerParams(vmem_limit_bytes=40 * 1024 * 1024)
EXCITE, RESPONSE, TABLE, ROWS = 0, 1024, 1280, 1296


def call(kernel, out_shape, in_specs, name, flops=0, size=1 << 20, scratch=(), aliases=None, params=PARAMS, out_spec=VMEM):
    many = isinstance(out_shape, tuple)
    return pl.pallas_call(
        kernel,
        out_shape=out_shape,
        in_specs=in_specs,
        out_specs=tuple(out_spec for _ in out_shape) if many else out_spec,
        scratch_shapes=list(scratch),
        input_output_aliases=aliases or {},
        compiler_params=params,
        cost_estimate=pl.CostEstimate(flops=flops, bytes_accessed=size, transcendentals=0),
        name=name,
    )


def partner(at, shifted):
    odd = at % 2
    return (at + 1 - 2 * (odd ^ shifted)) % 4


def peer(y, x, d, shifted):
    return (partner(y, shifted) if d & 2 else y), (partner(x, shifted) if d & 1 else x)


A_UP = (0, 1, 0, 1, 0)
B_UP = (1, 0, 0, 1)


def step(value, k, up):
    perm = []
    for z in range(8):
        perm.append((2 * z + up[k - 1], 2 * ((z + 1) % 8) + up[k]))
        perm.append((2 * z + 1 - up[k - 1], 2 * ((z - 1) % 8) + 1 - up[k]))
    return lax.ppermute(value, "group", perm)


def locate(region, me):
    core, kind = me % 2, region % 2
    below = (me // 2 - region // 2) % 8
    slot = jnp.where(kind == core, 0, 8)
    for k in range(1, 5):
        for way, steps in ((0, below), (1, 8 - below)):
            on = A_UP[k] ^ way
            here = (steps == k) & (kind == way)
            slot = jnp.where(here, jnp.where(core == on, k if k < 4 else 7, 8 if k < 4 else 9), slot)
            if k < 4:
                on = B_UP[k] ^ way
                here = (steps == k) & (kind != way)
                slot = jnp.where(here, jnp.where(core == on, 3 + k, 8), slot)
    return slot


def pick_kernel(pair_ref, *refs):
    regions, out_ref = refs[:7], refs[7]
    me = lax.axis_index("group")
    pair = pair_ref[...]
    for n in range(2):
        slot = locate(pair[0, n], me)
        for k, ref in enumerate(regions):

            @pl.when(slot == k)
            def _(ref=ref):
                out_ref[n] = ref[...]


def split3(x):
    first = x.astype(BF)
    rest = x - first.astype(F32)
    second = rest.astype(BF)
    third = (rest - second.astype(F32)).astype(BF)
    return first.astype(F32), second.astype(F32), third.astype(F32)


def prepare_kernel(shapes_ref, omega_ref, damping_ref, own_ref, table_ref):
    own_ref[...] = shapes_ref[:, 0]
    pieces = split3(omega_ref[...]) + split3(damping_ref[...])
    rows = lax.broadcasted_iota(jnp.int32, (16, 128), 0)
    table = jnp.zeros((16, 128), F32)
    for n, piece in enumerate(pieces):
        table = jnp.where(rows == n, piece, table)
    table_ref[...] = table.astype(BF)


def fan_kernel(pair_ref, table_ref, *refs):
    regions, other_ref, far_ref, out_refs, picked_ref = refs[:8], refs[8], refs[9], refs[10:14], refs[14]
    me = lax.axis_index("group")
    pair = pair_ref[...]
    for n in range(2):
        slot = locate(pair[0, n], me)
        for k, ref in enumerate(regions + (other_ref.at[n], far_ref)):

            @pl.when(slot == k)
            def _(ref=ref):
                picked_ref[n] = ref[...]

    core = me % 2
    at_mode = lax.axis_index("mode")
    for d, out_ref in enumerate(out_refs):
        y, x = peer(at_mode // 4, at_mode % 4, d, 1 - core)
        out_ref[EXCITE : EXCITE + 512, :] = picked_ref[1, 0]
        out_ref[EXCITE + 512 : EXCITE + 1024, :] = picked_ref[1, 1]
        for e in range(4):
            owner_y, owner_x = peer(y, x, e, core)
            owned = pl.ds(pl.multiple_of(32 * (4 * owner_y + owner_x), 32), 32)
            at = RESPONSE + 32 * e
            out_ref[at : at + 32, :] = picked_ref[0, 0, owned, :]
            out_ref[at + 128 : at + 160, :] = picked_ref[0, 1, owned, :]
        out_ref[TABLE:ROWS, :] = table_ref[...]


def weights(table, speed):
    omega = table[0:1] + table[1:2] + table[2:3]
    damping = table[3:4] + table[4:5] + table[5:6]
    a = omega * omega - speed * speed
    b = 2.0 * damping * omega * speed
    denom = a * a + b * b
    return a / denom, -b / denom


def share(parts, speeds_ref):
    left, modes = [], []
    for ref in parts:
        res_re = ref[RESPONSE : RESPONSE + 128, :]
        res_im = ref[RESPONSE + 128 : RESPONSE + 256, :]
        left.append(jnp.concatenate([res_re, res_im], axis=0))
        left.append(jnp.concatenate([-res_im, res_re], axis=0))
        modes.append(ref[TABLE:ROWS, :].astype(F32))
    left = jnp.concatenate(left, axis=1)
    for s in range(4):
        right = []
        for ref, table in zip(parts, modes):
            wre, wim = weights(table, speeds_ref[s : s + 1, :])
            ere = ref[EXCITE : EXCITE + 512, :].astype(F32)
            eim = ref[EXCITE + 512 : EXCITE + 1024, :].astype(F32)
            right.append((wre * ere - wim * eim).astype(BF))
            right.append((wre * eim + wim * ere).astype(BF))
        right = jnp.concatenate(right, axis=1)
        yield s, lax.dot_general(
            left, right, (((1,), (1,)), ((), ())), preferred_element_type=F32
        )


def first_kernel(part_ref, speeds_ref, out_ref, speed_rows_ref):
    rows = lax.broadcasted_iota(jnp.int32, (8, 128), 0)
    speeds = jnp.zeros((8, 128), F32)
    for s in range(4):
        speeds = jnp.where(rows == s, speeds_ref[s], speeds)
    speed_rows_ref[...] = speeds
    for s, both in share([part_ref], speed_rows_ref):
        out_ref[s] = both


def next_kernel(total_ref, part_ref, speeds_ref, out_ref):
    for s, both in share([part_ref], speeds_ref):
        out_ref[s] = total_ref[s] + both


def last_kernel(total_ref, part_ref, other_ref, speeds_ref, own_ref, *out_refs):
    parts = (part_ref, other_ref)
    right, modes = [], []
    for ref in parts:
        right.append(ref[EXCITE : EXCITE + 512, :])
        right.append(ref[EXCITE + 512 : EXCITE + 1024, :])
        modes.append(ref[TABLE:ROWS, :].astype(F32))
    right = jnp.concatenate(right, axis=1)
    for s in range(4):
        left = []
        for ref, table in zip(parts, modes):
            wre, wim = weights(table, speeds_ref[s : s + 1, :])
            rre = ref[RESPONSE : RESPONSE + 128, :].astype(F32)
            rim = ref[RESPONSE + 128 : RESPONSE + 256, :].astype(F32)
            lre = wre * rre - wim * rim
            lim = wre * rim + wim * rre
            left.append(jnp.concatenate([lre, lim], axis=0).astype(BF))
            left.append(jnp.concatenate([-lim, lre], axis=0).astype(BF))
        both = total_ref[s] + lax.dot_general(
            jnp.concatenate(left, axis=1),
            right,
            (((1,), (1,)), ((), ())),
            preferred_element_type=F32,
        )
        for c in range(2):
            at = (2 * s + c) * 512
            own_ref[:, at : at + 512] = both[128 * c : 128 * c + 32]
            for e in range(1, 4):
                row = 128 * c + 32 * e
                out_refs[e - 1][:, at : at + 512] = both[row : row + 32].astype(BF)


def sum_kernel(*refs):
    terms, out_ref = refs[:4], refs[4]
    for s in range(4):
        for c in range(2):
            at = (2 * s + c) * 512
            total = terms[0][:, at : at + 512]
            for ref in terms[1:]:
                total = total + ref[:, at : at + 512].astype(F32)
            out_ref[:, 0, s, c, :] = total


def exchange(value, d, flip):
    perm = []
    for g in range(16):
        for m in range(16):
            y, x = peer(m // 4, m % 4, d, 1 ^ (g % 2) ^ flip)
            perm.append((16 * g + m, 16 * g + 4 * y + x))
    return lax.ppermute(value, ("group", "mode"), perm)


def swap_cores(value):
    return lax.ppermute(value, "group", [(g, g ^ 1) for g in range(16)])


def shards(shapes, pairs, omega, damping, speeds):
    a1 = step(shapes.reshape(2, 512, 128), 1, A_UP)
    own, table = call(
        prepare_kernel,
        (jax.ShapeDtypeStruct((2, 512, 128), BF), jax.ShapeDtypeStruct((16, 128), BF)),
        [VMEM] * 3,
        "prepare",
    )(shapes, omega.reshape(1, 128), damping.reshape(1, 128))
    b1 = step(own, 1, B_UP)
    a1, other_pair = lax.optimization_barrier((a1, swap_cores(pairs)))
    a2 = step(a1, 2, A_UP)
    b2 = step(b1, 2, B_UP)
    a3 = step(a2, 3, A_UP)
    b3 = step(b2, 3, B_UP)
    a4 = step(a3, 4, A_UP)
    regions = (own, a1, a2, a3, b1, b2, b3)
    other = jax.ShapeDtypeStruct((2, 2, 512, 128), BF)
    wanted = call(pick_kernel, other, [VMEM] * 8, "pick_regions")(other_pair, *regions)
    message = jax.ShapeDtypeStruct((ROWS, 128), BF)
    fanned = call(
        fan_kernel,
        (message,) * 4,
        [VMEM] * 12,
        "fan_out",
        scratch=[pltpu.VMEM((2, 2, 512, 128), BF)],
    )(pairs, table, *regions, a4, swap_cores(wanted), swap_cores(a4))
    parts = [fanned[0]] + [exchange(fanned[d], d, 0) for d in (3, 2, 1)]
    sums = jax.ShapeDtypeStruct((4, 256, 512), F32)
    total, speed_rows = call(
        first_kernel,
        (sums, jax.ShapeDtypeStruct((8, 128), F32)),
        [VMEM, SMEM],
        "product_0",
        flops=1 << 28,
    )(parts[0], speeds)
    total = call(
        next_kernel, sums, [VMEM] * 3, "product_1", flops=1 << 28, aliases={0: 0}
    )(total, parts[1], speed_rows)
    block = jax.ShapeDtypeStruct((32, 4096), BF)
    made = call(
        last_kernel,
        (jax.ShapeDtypeStruct((32, 4096), F32), block, block, block),
        [VMEM] * 4,
        "product_2",
        flops=1 << 29,
    )(total, parts[2], parts[3], speed_rows)
    terms = [made[0]] + [exchange(made[e], e, 1) for e in (3, 2, 1)]
    return call(
        sum_kernel, jax.ShapeDtypeStruct((32, 1, 4, 2, 512), F32), [VMEM] * 4, "sum_terms"
    )(*terms)


def solution(mesh):
    in_specs = (P(None, "group", None, "mode"), P("group", None), P("mode"), P("mode"), P())
    out_specs = P("mode", "group", None, None, None)
    return jax.shard_map(shards, mesh=mesh, in_specs=in_specs, out_specs=out_specs, check_vma=False)
```

```python
import jax
import jax.numpy as jnp
from jax import lax
from jax.experimental import pallas as pl
from jax.experimental.pallas import tpu as pltpu
from jax.sharding import PartitionSpec as P

BF = jnp.bfloat16
F32 = jnp.float32
VMEM = pl.BlockSpec(memory_space=pltpu.VMEM)
SMEM = pl.BlockSpec(memory_space=pltpu.SMEM)
HBM = pl.BlockSpec(memory_space=pltpu.HBM)
PARAMS = pltpu.CompilerParams(vmem_limit_bytes=40 * 1024 * 1024)
EXCITE, RESPONSE, TABLE, ROWS = 0, 1024, 1280, 1296


def call(kernel, out_shape, in_specs, name, flops=0, size=1 << 20, scratch=(), aliases=None, params=PARAMS, out_spec=VMEM):
    many = isinstance(out_shape, tuple)
    return pl.pallas_call(
        kernel,
        out_shape=out_shape,
        in_specs=in_specs,
        out_specs=tuple(out_spec for _ in out_shape) if many else out_spec,
        scratch_shapes=list(scratch),
        input_output_aliases=aliases or {},
        compiler_params=params,
        cost_estimate=pl.CostEstimate(flops=flops, bytes_accessed=size, transcendentals=0),
        name=name,
    )


def partner(at, shifted):
    odd = at % 2
    return (at + 1 - 2 * (odd ^ shifted)) % 4


def peer(y, x, d, shifted):
    return (partner(y, shifted) if d & 2 else y), (partner(x, shifted) if d & 1 else x)


A_UP = (0, 1, 0, 1, 0)
B_UP = (1, 0, 0, 1)


def step(value, k, up):
    perm = []
    for z in range(8):
        perm.append((2 * z + up[k - 1], 2 * ((z + 1) % 8) + up[k]))
        perm.append((2 * z + 1 - up[k - 1], 2 * ((z - 1) % 8) + 1 - up[k]))
    return lax.ppermute(value, "group", perm)


def locate(region, me):
    core, kind = me % 2, region % 2
    below = (me // 2 - region // 2) % 8
    slot = jnp.where(kind == core, 0, 8)
    for k in range(1, 5):
        for way, steps in ((0, below), (1, 8 - below)):
            on = A_UP[k] ^ way
            here = (steps == k) & (kind == way)
            slot = jnp.where(here, jnp.where(core == on, k if k < 4 else 7, 8 if k < 4 else 9), slot)
            if k < 4:
                on = B_UP[k] ^ way
                here = (steps == k) & (kind != way)
                slot = jnp.where(here, jnp.where(core == on, 3 + k, 8), slot)
    return slot


def pick_kernel(pair_ref, *refs):
    regions, out_ref = refs[:7], refs[7]
    me = lax.axis_index("group")
    pair = pair_ref[...]
    for n in range(2):
        slot = locate(pair[0, n], me)
        for k, ref in enumerate(regions):

            @pl.when(slot == k)
            def _(ref=ref):
                out_ref[n] = ref[...]


def split3(x):
    first = x.astype(BF)
    rest = x - first.astype(F32)
    second = rest.astype(BF)
    third = (rest - second.astype(F32)).astype(BF)
    return first.astype(F32), second.astype(F32), third.astype(F32)


def prepare_kernel(shapes_ref, omega_ref, damping_ref, own_ref, table_ref):
    own_ref[...] = shapes_ref[:, 0]
    pieces = split3(omega_ref[...]) + split3(damping_ref[...])
    rows = lax.broadcasted_iota(jnp.int32, (16, 128), 0)
    table = jnp.zeros((16, 128), F32)
    for n, piece in enumerate(pieces):
        table = jnp.where(rows == n, piece, table)
    table_ref[...] = table.astype(BF)


def fan_kernel(pair_ref, table_ref, *refs):
    regions, other_ref, far_ref, out_refs, picked_ref = refs[:8], refs[8], refs[9], refs[10:14], refs[14]
    me = lax.axis_index("group")
    pair = pair_ref[...]
    for n in range(2):
        slot = locate(pair[0, n], me)
        for k, ref in enumerate(regions + (other_ref.at[n], far_ref)):

            @pl.when(slot == k)
            def _(ref=ref):
                picked_ref[n] = ref[...]

    core = me % 2
    at_mode = lax.axis_index("mode")
    for d, out_ref in enumerate(out_refs):
        y, x = peer(at_mode // 4, at_mode % 4, d, 1 - core)
        out_ref[EXCITE : EXCITE + 512, :] = picked_ref[1, 0]
        out_ref[EXCITE + 512 : EXCITE + 1024, :] = picked_ref[1, 1]
        for e in range(4):
            owner_y, owner_x = peer(y, x, e, core)
            owned = pl.ds(pl.multiple_of(32 * (4 * owner_y + owner_x), 32), 32)
            at = RESPONSE + 32 * e
            out_ref[at : at + 32, :] = picked_ref[0, 0, owned, :]
            out_ref[at + 128 : at + 160, :] = picked_ref[0, 1, owned, :]
        out_ref[TABLE:ROWS, :] = table_ref[...]


def weights(table, speed):
    omega = table[0:1] + table[1:2] + table[2:3]
    damping = table[3:4] + table[4:5] + table[5:6]
    a = omega * omega - speed * speed
    b = 2.0 * damping * omega * speed
    denom = a * a + b * b
    return a / denom, -b / denom


def share(parts, speeds_ref):
    left, modes = [], []
    for ref in parts:
        res_re = ref[RESPONSE : RESPONSE + 128, :]
        res_im = ref[RESPONSE + 128 : RESPONSE + 256, :]
        left.append(jnp.concatenate([res_re, res_im], axis=0))
        left.append(jnp.concatenate([-res_im, res_re], axis=0))
        modes.append(ref[TABLE:ROWS, :].astype(F32))
    left = jnp.concatenate(left, axis=1)
    for s in range(4):
        right = []
        for ref, table in zip(parts, modes):
            wre, wim = weights(table, speeds_ref[s : s + 1, :])
            ere = ref[EXCITE : EXCITE + 512, :].astype(F32)
            eim = ref[EXCITE + 512 : EXCITE + 1024, :].astype(F32)
            right.append((wre * ere - wim * eim).astype(BF))
            right.append((wre * eim + wim * ere).astype(BF))
        right = jnp.concatenate(right, axis=1)
        yield s, lax.dot_general(
            left, right, (((1,), (1,)), ((), ())), preferred_element_type=F32
        )


def first_kernel(part_ref, speeds_ref, out_ref, speed_rows_ref):
    rows = lax.broadcasted_iota(jnp.int32, (8, 128), 0)
    speeds = jnp.zeros((8, 128), F32)
    for s in range(4):
        speeds = jnp.where(rows == s, speeds_ref[s], speeds)
    speed_rows_ref[...] = speeds
    for s, both in share([part_ref], speed_rows_ref):
        out_ref[s] = both


def next_kernel(total_ref, part_ref, speeds_ref, out_ref):
    for s, both in share([part_ref], speeds_ref):
        out_ref[s] = total_ref[s] + both


def last_kernel(total_ref, part_ref, other_ref, speeds_ref, own_ref, *out_refs):
    parts = (part_ref, other_ref)
    right, modes = [], []
    for ref in parts:
        right.append(ref[EXCITE : EXCITE + 512, :])
        right.append(ref[EXCITE + 512 : EXCITE + 1024, :])
        modes.append(ref[TABLE:ROWS, :].astype(F32))
    right = jnp.concatenate(right, axis=1)
    for s in range(4):
        left = []
        for ref, table in zip(parts, modes):
            wre, wim = weights(table, speeds_ref[s : s + 1, :])
            rre = ref[RESPONSE : RESPONSE + 128, :].astype(F32)
            rim = ref[RESPONSE + 128 : RESPONSE + 256, :].astype(F32)
            lre = wre * rre - wim * rim
            lim = wre * rim + wim * rre
            left.append(jnp.concatenate([lre, lim], axis=0).astype(BF))
            left.append(jnp.concatenate([-lim, lre], axis=0).astype(BF))
        both = total_ref[s] + lax.dot_general(
            jnp.concatenate(left, axis=1),
            right,
            (((1,), (1,)), ((), ())),
            preferred_element_type=F32,
        )
        for c in range(2):
            at = (2 * s + c) * 512
            own_ref[:, at : at + 512] = both[128 * c : 128 * c + 32]
            for e in range(1, 4):
                row = 128 * c + 32 * e
                out_refs[e - 1][:, at : at + 512] = both[row : row + 32].astype(BF)


def sum_kernel(*refs):
    terms, out_ref, total_ref, sems = refs[:4], refs[4], refs[5], refs[6]
    copies = []
    for q in range(4):
        rows = slice(8 * q, 8 * q + 8)
        for s in range(4):
            for c in range(2):
                at = (2 * s + c) * 512
                total = terms[0][rows, at : at + 512]
                for ref in terms[1:]:
                    total = total + ref[rows, at : at + 512].astype(F32)
                total_ref[rows, s, c, :] = total
        copy = pltpu.make_async_copy(total_ref.at[rows], out_ref.at[rows, 0], sems.at[q])
        copy.start()
        copies.append(copy)
    for copy in copies:
        copy.wait()


def exchange(value, d, flip):
    perm = []
    for g in range(16):
        for m in range(16):
            y, x = peer(m // 4, m % 4, d, 1 ^ (g % 2) ^ flip)
            perm.append((16 * g + m, 16 * g + 4 * y + x))
    return lax.ppermute(value, ("group", "mode"), perm)


def swap_cores(value):
    return lax.ppermute(value, "group", [(g, g ^ 1) for g in range(16)])


def shards(shapes, pairs, omega, damping, speeds):
    a1 = step(shapes.reshape(2, 512, 128), 1, A_UP)
    own, table = call(
        prepare_kernel,
        (jax.ShapeDtypeStruct((2, 512, 128), BF), jax.ShapeDtypeStruct((16, 128), BF)),
        [VMEM] * 3,
        "prepare",
    )(shapes, omega.reshape(1, 128), damping.reshape(1, 128))
    b1 = step(own, 1, B_UP)
    a2 = step(a1, 2, A_UP)
    b2 = step(b1, 2, B_UP)
    a3 = step(a2, 3, A_UP)
    b3 = step(b2, 3, B_UP)
    a4 = step(a3, 4, A_UP)
    regions = (own, a1, a2, a3, b1, b2, b3)
    other = jax.ShapeDtypeStruct((2, 2, 512, 128), BF)
    wanted = call(pick_kernel, other, [VMEM] * 8, "pick_regions")(swap_cores(pairs), *regions)
    message = jax.ShapeDtypeStruct((ROWS, 128), BF)
    fanned = call(
        fan_kernel,
        (message,) * 4,
        [VMEM] * 12,
        "fan_out",
        scratch=[pltpu.VMEM((2, 2, 512, 128), BF)],
    )(pairs, table, *regions, a4, swap_cores(wanted), swap_cores(a4))
    parts = [fanned[0]] + [exchange(fanned[d], d, 0) for d in (3, 2, 1)]
    sums = jax.ShapeDtypeStruct((4, 256, 512), F32)
    total, speed_rows = call(
        first_kernel,
        (sums, jax.ShapeDtypeStruct((8, 128), F32)),
        [VMEM, SMEM],
        "product_0",
        flops=1 << 28,
    )(parts[0], speeds)
    total = call(
        next_kernel, sums, [VMEM] * 3, "product_1", flops=1 << 28, aliases={0: 0}
    )(total, parts[1], speed_rows)
    block = jax.ShapeDtypeStruct((32, 4096), BF)
    made = call(
        last_kernel,
        (jax.ShapeDtypeStruct((32, 4096), F32), block, block, block),
        [VMEM] * 4,
        "product_2",
        flops=1 << 29,
    )(total, parts[2], parts[3], speed_rows)
    terms = [made[0]] + [exchange(made[e], e, 1) for e in (3, 2, 1)]
    return call(
        sum_kernel,
        jax.ShapeDtypeStruct((32, 1, 4, 2, 512), F32),
        [VMEM] * 4,
        "sum_terms",
        scratch=[pltpu.VMEM((32, 4, 2, 512), F32), pltpu.SemaphoreType.DMA((4,))],
        out_spec=HBM,
    )(*terms)


def solution(mesh):
    in_specs = (P(None, "group", None, "mode"), P("group", None), P("mode"), P("mode"), P())
    out_specs = P("mode", "group", None, None, None)
    return jax.shard_map(shards, mesh=mesh, in_specs=in_specs, out_specs=out_specs, check_vma=False)
```

```python
import jax
import jax.numpy as jnp
from jax import lax
from jax.experimental import pallas as pl
from jax.experimental.pallas import tpu as pltpu
from jax.sharding import PartitionSpec as P

BF = jnp.bfloat16
F32 = jnp.float32
VMEM = pl.BlockSpec(memory_space=pltpu.VMEM)
SMEM = pl.BlockSpec(memory_space=pltpu.SMEM)
HBM = pl.BlockSpec(memory_space=pltpu.HBM)
PARAMS = pltpu.CompilerParams(vmem_limit_bytes=40 * 1024 * 1024)
EXCITE, RESPONSE, TABLE, ROWS = 0, 1024, 1280, 1296


def call(kernel, out_shape, in_specs, name, flops=0, size=1 << 20, scratch=(), aliases=None, params=PARAMS, out_spec=VMEM):
    many = isinstance(out_shape, tuple)
    return pl.pallas_call(
        kernel,
        out_shape=out_shape,
        in_specs=in_specs,
        out_specs=tuple(out_spec for _ in out_shape) if many else out_spec,
        scratch_shapes=list(scratch),
        input_output_aliases=aliases or {},
        compiler_params=params,
        cost_estimate=pl.CostEstimate(flops=flops, bytes_accessed=size, transcendentals=0),
        name=name,
    )


def partner(at, shifted):
    odd = at % 2
    return (at + 1 - 2 * (odd ^ shifted)) % 4


def peer(y, x, d, shifted):
    return (partner(y, shifted) if d & 2 else y), (partner(x, shifted) if d & 1 else x)


A_UP = (0, 1, 0, 1, 0)
B_UP = (1, 0, 0, 1)


def step(value, k, up):
    perm = []
    for z in range(8):
        perm.append((2 * z + up[k - 1], 2 * ((z + 1) % 8) + up[k]))
        perm.append((2 * z + 1 - up[k - 1], 2 * ((z - 1) % 8) + 1 - up[k]))
    return lax.ppermute(value, "group", perm)


def locate(region, me):
    core, kind = me % 2, region % 2
    below = (me // 2 - region // 2) % 8
    slot = jnp.where(kind == core, 0, 8)
    for k in range(1, 5):
        for way, steps in ((0, below), (1, 8 - below)):
            on = A_UP[k] ^ way
            here = (steps == k) & (kind == way)
            slot = jnp.where(here, jnp.where(core == on, k if k < 4 else 7, 8 if k < 4 else 9), slot)
            if k < 4:
                on = B_UP[k] ^ way
                here = (steps == k) & (kind != way)
                slot = jnp.where(here, jnp.where(core == on, 3 + k, 8), slot)
    return slot


def pick_kernel(pair_ref, *refs):
    regions, out_ref = refs[:7], refs[7]
    me = lax.axis_index("group")
    pair = pair_ref[...]
    for n in range(2):
        slot = locate(pair[0, n], me)
        for k, ref in enumerate(regions):

            @pl.when(slot == k)
            def _(ref=ref):
                out_ref[n] = ref[...]


def split3(x):
    first = x.astype(BF)
    rest = x - first.astype(F32)
    second = rest.astype(BF)
    third = (rest - second.astype(F32)).astype(BF)
    return first.astype(F32), second.astype(F32), third.astype(F32)


def prepare_kernel(shapes_ref, omega_ref, damping_ref, own_ref, table_ref):
    own_ref[...] = shapes_ref[:, 0]
    pieces = split3(omega_ref[...]) + split3(damping_ref[...])
    rows = lax.broadcasted_iota(jnp.int32, (16, 128), 0)
    table = jnp.zeros((16, 128), F32)
    for n, piece in enumerate(pieces):
        table = jnp.where(rows == n, piece, table)
    table_ref[...] = table.astype(BF)


def fan_kernel(pair_ref, table_ref, *refs):
    regions, other_ref, far_ref, out_refs, picked_ref = refs[:8], refs[8], refs[9], refs[10:14], refs[14]
    me = lax.axis_index("group")
    pair = pair_ref[...]
    for n in range(2):
        slot = locate(pair[0, n], me)
        for k, ref in enumerate(regions + (other_ref.at[n], far_ref)):

            @pl.when(slot == k)
            def _(ref=ref):
                picked_ref[n] = ref[...]

    core = me % 2
    at_mode = lax.axis_index("mode")
    for d, out_ref in enumerate(out_refs):
        y, x = peer(at_mode // 4, at_mode % 4, d, 1 - core)
        out_ref[EXCITE : EXCITE + 512, :] = picked_ref[1, 0]
        out_ref[EXCITE + 512 : EXCITE + 1024, :] = picked_ref[1, 1]
        for e in range(4):
            owner_y, owner_x = peer(y, x, e, core)
            owned = pl.ds(pl.multiple_of(32 * (4 * owner_y + owner_x), 32), 32)
            at = RESPONSE + 32 * e
            out_ref[at : at + 32, :] = picked_ref[0, 0, owned, :]
            out_ref[at + 128 : at + 160, :] = picked_ref[0, 1, owned, :]
        out_ref[TABLE:ROWS, :] = table_ref[...]


def weights(table, speed):
    omega = table[0:1] + table[1:2] + table[2:3]
    damping = table[3:4] + table[4:5] + table[5:6]
    a = omega * omega - speed * speed
    b = 2.0 * damping * omega * speed
    denom = a * a + b * b
    return a / denom, -b / denom


def share(parts, speeds_ref):
    left, modes = [], []
    for ref in parts:
        res_re = ref[RESPONSE : RESPONSE + 128, :]
        res_im = ref[RESPONSE + 128 : RESPONSE + 256, :]
        left.append(jnp.concatenate([res_re, res_im], axis=0))
        left.append(jnp.concatenate([-res_im, res_re], axis=0))
        modes.append(ref[TABLE:ROWS, :].astype(F32))
    left = jnp.concatenate(left, axis=1)
    for s in range(4):
        right = []
        for ref, table in zip(parts, modes):
            wre, wim = weights(table, speeds_ref[s : s + 1, :])
            ere = ref[EXCITE : EXCITE + 512, :].astype(F32)
            eim = ref[EXCITE + 512 : EXCITE + 1024, :].astype(F32)
            right.append((wre * ere - wim * eim).astype(BF))
            right.append((wre * eim + wim * ere).astype(BF))
        right = jnp.concatenate(right, axis=1)
        yield s, lax.dot_general(
            left, right, (((1,), (1,)), ((), ())), preferred_element_type=F32
        )


def first_kernel(part_ref, speeds_ref, out_ref, speed_rows_ref):
    rows = lax.broadcasted_iota(jnp.int32, (8, 128), 0)
    speeds = jnp.zeros((8, 128), F32)
    for s in range(4):
        speeds = jnp.where(rows == s, speeds_ref[s], speeds)
    speed_rows_ref[...] = speeds
    for s, both in share([part_ref], speed_rows_ref):
        out_ref[s] = both


def next_kernel(total_ref, part_ref, speeds_ref, out_ref):
    for s, both in share([part_ref], speeds_ref):
        out_ref[s] = total_ref[s] + both


def last_kernel(total_ref, part_ref, other_ref, speeds_ref, own_ref, *out_refs):
    parts = (part_ref, other_ref)
    right, modes = [], []
    for ref in parts:
        right.append(ref[EXCITE : EXCITE + 512, :])
        right.append(ref[EXCITE + 512 : EXCITE + 1024, :])
        modes.append(ref[TABLE:ROWS, :].astype(F32))
    right = jnp.concatenate(right, axis=1)
    for s in range(4):
        left = []
        for ref, table in zip(parts, modes):
            wre, wim = weights(table, speeds_ref[s : s + 1, :])
            rre = ref[RESPONSE : RESPONSE + 128, :].astype(F32)
            rim = ref[RESPONSE + 128 : RESPONSE + 256, :].astype(F32)
            lre = wre * rre - wim * rim
            lim = wre * rim + wim * rre
            left.append(jnp.concatenate([lre, lim], axis=0).astype(BF))
            left.append(jnp.concatenate([-lim, lre], axis=0).astype(BF))
        both = total_ref[s] + lax.dot_general(
            jnp.concatenate(left, axis=1),
            right,
            (((1,), (1,)), ((), ())),
            preferred_element_type=F32,
        )
        for c in range(2):
            at = (2 * s + c) * 512
            own_ref[:, at : at + 512] = both[128 * c : 128 * c + 32]
            for e in range(1, 4):
                row = 128 * c + 32 * e
                out_refs[e - 1][:, at : at + 512] = both[row : row + 32].astype(BF)


def sum_kernel(*refs):
    terms, out_ref, total_ref, sems = refs[:4], refs[4], refs[5], refs[6]
    copies = []
    for q in range(2):
        rows = slice(16 * q, 16 * q + 16)
        for s in range(4):
            for c in range(2):
                at = (2 * s + c) * 512
                total = terms[0][rows, at : at + 512]
                for ref in terms[1:]:
                    total = total + ref[rows, at : at + 512].astype(F32)
                total_ref[rows, s, c, :] = total
        copy = pltpu.make_async_copy(total_ref.at[rows], out_ref.at[rows, 0], sems.at[q])
        copy.start()
        copies.append(copy)
    for copy in copies:
        copy.wait()


def exchange(value, d, flip):
    perm = []
    for g in range(16):
        for m in range(16):
            y, x = peer(m // 4, m % 4, d, 1 ^ (g % 2) ^ flip)
            perm.append((16 * g + m, 16 * g + 4 * y + x))
    return lax.ppermute(value, ("group", "mode"), perm)


def swap_cores(value):
    return lax.ppermute(value, "group", [(g, g ^ 1) for g in range(16)])


def shards(shapes, pairs, omega, damping, speeds):
    a1 = step(shapes.reshape(2, 512, 128), 1, A_UP)
    own, table = call(
        prepare_kernel,
        (jax.ShapeDtypeStruct((2, 512, 128), BF), jax.ShapeDtypeStruct((16, 128), BF)),
        [VMEM] * 3,
        "prepare",
    )(shapes, omega.reshape(1, 128), damping.reshape(1, 128))
    b1 = step(own, 1, B_UP)
    a2 = step(a1, 2, A_UP)
    b2 = step(b1, 2, B_UP)
    a3 = step(a2, 3, A_UP)
    b3 = step(b2, 3, B_UP)
    a4 = step(a3, 4, A_UP)
    regions = (own, a1, a2, a3, b1, b2, b3)
    other = jax.ShapeDtypeStruct((2, 2, 512, 128), BF)
    wanted = call(pick_kernel, other, [VMEM] * 8, "pick_regions")(swap_cores(pairs), *regions)
    message = jax.ShapeDtypeStruct((ROWS, 128), BF)
    fanned = call(
        fan_kernel,
        (message,) * 4,
        [VMEM] * 12,
        "fan_out",
        scratch=[pltpu.VMEM((2, 2, 512, 128), BF)],
    )(pairs, table, *regions, a4, swap_cores(wanted), swap_cores(a4))
    parts = [fanned[0]] + [exchange(fanned[d], d, 0) for d in (3, 2, 1)]
    sums = jax.ShapeDtypeStruct((4, 256, 512), F32)
    total, speed_rows = call(
        first_kernel,
        (sums, jax.ShapeDtypeStruct((8, 128), F32)),
        [VMEM, SMEM],
        "product_0",
        flops=1 << 28,
    )(parts[0], speeds)
    total = call(
        next_kernel, sums, [VMEM] * 3, "product_1", flops=1 << 28, aliases={0: 0}
    )(total, parts[1], speed_rows)
    block = jax.ShapeDtypeStruct((32, 4096), BF)
    made = call(
        last_kernel,
        (jax.ShapeDtypeStruct((32, 4096), F32), block, block, block),
        [VMEM] * 4,
        "product_2",
        flops=1 << 29,
    )(total, parts[2], parts[3], speed_rows)
    terms = [made[0]] + [exchange(made[e], e, 1) for e in (3, 2, 1)]
    return call(
        sum_kernel,
        jax.ShapeDtypeStruct((32, 1, 4, 2, 512), F32),
        [VMEM] * 4,
        "sum_terms",
        scratch=[pltpu.VMEM((32, 4, 2, 512), F32), pltpu.SemaphoreType.DMA((2,))],
        out_spec=HBM,
    )(*terms)


def solution(mesh):
    in_specs = (P(None, "group", None, "mode"), P("group", None), P("mode"), P("mode"), P())
    out_specs = P("mode", "group", None, None, None)
    return jax.shard_map(shards, mesh=mesh, in_specs=in_specs, out_specs=out_specs, check_vma=False)
```

```python
import jax
import jax.numpy as jnp
from jax import lax
from jax.experimental import pallas as pl
from jax.experimental.pallas import tpu as pltpu
from jax.sharding import PartitionSpec as P

BF = jnp.bfloat16
F32 = jnp.float32
VMEM = pl.BlockSpec(memory_space=pltpu.VMEM)
SMEM = pl.BlockSpec(memory_space=pltpu.SMEM)
HBM = pl.BlockSpec(memory_space=pltpu.HBM)
PARAMS = pltpu.CompilerParams(vmem_limit_bytes=40 * 1024 * 1024)
EXCITE, RESPONSE, TABLE, ROWS = 0, 1024, 1280, 1296


def call(kernel, out_shape, in_specs, name, flops=0, size=1 << 20, scratch=(), aliases=None, params=PARAMS, out_spec=VMEM):
    many = isinstance(out_shape, tuple)
    return pl.pallas_call(
        kernel,
        out_shape=out_shape,
        in_specs=in_specs,
        out_specs=tuple(out_spec for _ in out_shape) if many else out_spec,
        scratch_shapes=list(scratch),
        input_output_aliases=aliases or {},
        compiler_params=params,
        cost_estimate=pl.CostEstimate(flops=flops, bytes_accessed=size, transcendentals=0),
        name=name,
    )


def partner(at, shifted):
    odd = at % 2
    return (at + 1 - 2 * (odd ^ shifted)) % 4


def peer(y, x, d, shifted):
    return (partner(y, shifted) if d & 2 else y), (partner(x, shifted) if d & 1 else x)


A_UP = (0, 1, 0, 1, 0)
B_UP = (1, 0, 0, 1)


def step(value, k, up):
    perm = []
    for z in range(8):
        perm.append((2 * z + up[k - 1], 2 * ((z + 1) % 8) + up[k]))
        perm.append((2 * z + 1 - up[k - 1], 2 * ((z - 1) % 8) + 1 - up[k]))
    return lax.ppermute(value, "group", perm)


def locate(region, me):
    core, kind = me % 2, region % 2
    below = (me // 2 - region // 2) % 8
    slot = jnp.where(kind == core, 0, 8)
    for k in range(1, 5):
        for way, steps in ((0, below), (1, 8 - below)):
            on = A_UP[k] ^ way
            here = (steps == k) & (kind == way)
            slot = jnp.where(here, jnp.where(core == on, k if k < 4 else 7, 8 if k < 4 else 9), slot)
            if k < 4:
                on = B_UP[k] ^ way
                here = (steps == k) & (kind != way)
                slot = jnp.where(here, jnp.where(core == on, 3 + k, 8), slot)
    return slot


def pick_kernel(pair_ref, *refs):
    regions, out_ref = refs[:7], refs[7]
    me = lax.axis_index("group")
    pair = pair_ref[...]
    for n in range(2):
        slot = locate(pair[0, n], me)
        for k, ref in enumerate(regions):

            @pl.when(slot == k)
            def _(ref=ref):
                out_ref[n] = ref[...]


def split3(x):
    first = x.astype(BF)
    rest = x - first.astype(F32)
    second = rest.astype(BF)
    third = (rest - second.astype(F32)).astype(BF)
    return first.astype(F32), second.astype(F32), third.astype(F32)


def prepare_kernel(shapes_ref, omega_ref, damping_ref, own_ref, table_ref):
    own_ref[...] = shapes_ref[:, 0]
    pieces = split3(omega_ref[...]) + split3(damping_ref[...])
    rows = lax.broadcasted_iota(jnp.int32, (16, 128), 0)
    table = jnp.zeros((16, 128), F32)
    for n, piece in enumerate(pieces):
        table = jnp.where(rows == n, piece, table)
    table_ref[...] = table.astype(BF)


def fan_kernel(pair_ref, table_ref, *refs):
    regions, other_ref, far_ref, out_refs, picked_ref = refs[:8], refs[8], refs[9], refs[10:14], refs[14]
    me = lax.axis_index("group")
    pair = pair_ref[...]
    for n in range(2):
        slot = locate(pair[0, n], me)
        for k, ref in enumerate(regions + (other_ref.at[n], far_ref)):

            @pl.when(slot == k)
            def _(ref=ref):
                picked_ref[n] = ref[...]

    core = me % 2
    at_mode = lax.axis_index("mode")
    for d, out_ref in enumerate(out_refs):
        y, x = peer(at_mode // 4, at_mode % 4, d, 1 - core)
        out_ref[EXCITE : EXCITE + 512, :] = picked_ref[1, 0]
        out_ref[EXCITE + 512 : EXCITE + 1024, :] = picked_ref[1, 1]
        for e in range(4):
            owner_y, owner_x = peer(y, x, e, core)
            owned = pl.ds(pl.multiple_of(32 * (4 * owner_y + owner_x), 32), 32)
            at = RESPONSE + 32 * e
            out_ref[at : at + 32, :] = picked_ref[0, 0, owned, :]
            out_ref[at + 128 : at + 160, :] = picked_ref[0, 1, owned, :]
        out_ref[TABLE:ROWS, :] = table_ref[...]


def weights(table, speed):
    omega = table[0:1] + table[1:2] + table[2:3]
    damping = table[3:4] + table[4:5] + table[5:6]
    a = omega * omega - speed * speed
    b = 2.0 * damping * omega * speed
    denom = a * a + b * b
    return a / denom, -b / denom


def share(parts, speeds_ref):
    left, modes = [], []
    for ref in parts:
        res_re = ref[RESPONSE : RESPONSE + 128, :]
        res_im = ref[RESPONSE + 128 : RESPONSE + 256, :]
        left.append(jnp.concatenate([res_re, res_im], axis=0))
        left.append(jnp.concatenate([-res_im, res_re], axis=0))
        modes.append(ref[TABLE:ROWS, :].astype(F32))
    left = jnp.concatenate(left, axis=1)
    for s in range(4):
        right = []
        for ref, table in zip(parts, modes):
            wre, wim = weights(table, speeds_ref[s : s + 1, :])
            ere = ref[EXCITE : EXCITE + 512, :].astype(F32)
            eim = ref[EXCITE + 512 : EXCITE + 1024, :].astype(F32)
            right.append((wre * ere - wim * eim).astype(BF))
            right.append((wre * eim + wim * ere).astype(BF))
        right = jnp.concatenate(right, axis=1)
        yield s, lax.dot_general(
            left, right, (((1,), (1,)), ((), ())), preferred_element_type=F32
        )


def first_kernel(part_ref, speeds_ref, out_ref, speed_rows_ref):
    rows = lax.broadcasted_iota(jnp.int32, (8, 128), 0)
    speeds = jnp.zeros((8, 128), F32)
    for s in range(4):
        speeds = jnp.where(rows == s, speeds_ref[s], speeds)
    speed_rows_ref[...] = speeds
    for s, both in share([part_ref], speed_rows_ref):
        out_ref[s] = both


def next_kernel(total_ref, part_ref, speeds_ref, out_ref):
    for s, both in share([part_ref], speeds_ref):
        out_ref[s] = total_ref[s] + both


def last_kernel(total_ref, part_ref, other_ref, speeds_ref, own_ref, *out_refs):
    parts = (part_ref, other_ref)
    right, modes = [], []
    for ref in parts:
        right.append(ref[EXCITE : EXCITE + 512, :])
        right.append(ref[EXCITE + 512 : EXCITE + 1024, :])
        modes.append(ref[TABLE:ROWS, :].astype(F32))
    right = jnp.concatenate(right, axis=1)
    for s in range(4):
        left = []
        for ref, table in zip(parts, modes):
            wre, wim = weights(table, speeds_ref[s : s + 1, :])
            rre = ref[RESPONSE : RESPONSE + 128, :].astype(F32)
            rim = ref[RESPONSE + 128 : RESPONSE + 256, :].astype(F32)
            lre = wre * rre - wim * rim
            lim = wre * rim + wim * rre
            left.append(jnp.concatenate([lre, lim], axis=0).astype(BF))
            left.append(jnp.concatenate([-lim, lre], axis=0).astype(BF))
        both = total_ref[s] + lax.dot_general(
            jnp.concatenate(left, axis=1),
            right,
            (((1,), (1,)), ((), ())),
            preferred_element_type=F32,
        )
        for c in range(2):
            at = (2 * s + c) * 512
            own_ref[:, at : at + 512] = both[128 * c : 128 * c + 32]
            for e in range(1, 4):
                row = 128 * c + 32 * e
                out_refs[e - 1][:, at : at + 512] = both[row : row + 32].astype(BF)


def sum_kernel(*refs):
    terms, out_ref, total_ref, sems = refs[:4], refs[4], refs[5], refs[6]
    copies = []
    for q in range(2):
        rows = slice(16 * q, 16 * q + 16)
        for s in range(4):
            for c in range(2):
                at = (2 * s + c) * 512
                total = terms[0][rows, at : at + 512]
                for ref in terms[1:]:
                    total = total + ref[rows, at : at + 512].astype(F32)
                total_ref[rows, s, c, :] = total
        copy = pltpu.make_async_copy(total_ref.at[rows], out_ref.at[rows, 0], sems.at[q])
        copy.start()
        copies.append(copy)
    for copy in copies:
        copy.wait()


def exchange(value, d, flip):
    perm = []
    for g in range(16):
        for m in range(16):
            y, x = peer(m // 4, m % 4, d, 1 ^ (g % 2) ^ flip)
            perm.append((16 * g + m, 16 * g + 4 * y + x))
    return lax.ppermute(value, ("group", "mode"), perm)


def swap_cores(value):
    return lax.ppermute(value, "group", [(g, g ^ 1) for g in range(16)])


def shards(shapes, pairs, omega, damping, speeds):
    a1 = step(shapes.reshape(2, 512, 128), 1, A_UP)
    own, table = call(
        prepare_kernel,
        (jax.ShapeDtypeStruct((2, 512, 128), BF), jax.ShapeDtypeStruct((16, 128), BF)),
        [VMEM] * 3,
        "prepare",
    )(shapes, omega.reshape(1, 128), damping.reshape(1, 128))
    b1 = step(own, 1, B_UP)
    a2 = step(a1, 2, A_UP)
    b2 = step(b1, 2, B_UP)
    a3 = step(a2, 3, A_UP)
    b3 = step(b2, 3, B_UP)
    a4 = step(a3, 4, A_UP)
    regions = (own, a1, a2, a3, b1, b2, b3)
    other = jax.ShapeDtypeStruct((2, 2, 512, 128), BF)
    wanted = call(pick_kernel, other, [VMEM] * 8, "pick_regions")(swap_cores(pairs), *regions)
    message = jax.ShapeDtypeStruct((ROWS, 128), BF)
    fanned = call(
        fan_kernel,
        (message,) * 4,
        [VMEM] * 12,
        "fan_out",
        scratch=[pltpu.VMEM((2, 2, 512, 128), BF)],
    )(pairs, table, *regions, a4, swap_cores(wanted), swap_cores(a4))
    parts = [fanned[0]] + [exchange(fanned[d], d, 0) for d in (3, 1, 2)]
    sums = jax.ShapeDtypeStruct((4, 256, 512), F32)
    total, speed_rows = call(
        first_kernel,
        (sums, jax.ShapeDtypeStruct((8, 128), F32)),
        [VMEM, SMEM],
        "product_0",
        flops=1 << 28,
    )(parts[0], speeds)
    total = call(
        next_kernel, sums, [VMEM] * 3, "product_1", flops=1 << 28, aliases={0: 0}
    )(total, parts[1], speed_rows)
    block = jax.ShapeDtypeStruct((32, 4096), BF)
    made = call(
        last_kernel,
        (jax.ShapeDtypeStruct((32, 4096), F32), block, block, block),
        [VMEM] * 4,
        "product_2",
        flops=1 << 29,
    )(total, parts[2], parts[3], speed_rows)
    terms = [made[0]] + [exchange(made[e], e, 1) for e in (3, 2, 1)]
    return call(
        sum_kernel,
        jax.ShapeDtypeStruct((32, 1, 4, 2, 512), F32),
        [VMEM] * 4,
        "sum_terms",
        scratch=[pltpu.VMEM((32, 4, 2, 512), F32), pltpu.SemaphoreType.DMA((2,))],
        out_spec=HBM,
    )(*terms)


def solution(mesh):
    in_specs = (P(None, "group", None, "mode"), P("group", None), P("mode"), P("mode"), P())
    out_specs = P("mode", "group", None, None, None)
    return jax.shard_map(shards, mesh=mesh, in_specs=in_specs, out_specs=out_specs, check_vma=False)
```

```python
import jax
import jax.numpy as jnp
from jax import lax
from jax.experimental import pallas as pl
from jax.experimental.pallas import tpu as pltpu
from jax.sharding import PartitionSpec as P

BF = jnp.bfloat16
F32 = jnp.float32
VMEM = pl.BlockSpec(memory_space=pltpu.VMEM)
SMEM = pl.BlockSpec(memory_space=pltpu.SMEM)
HBM = pl.BlockSpec(memory_space=pltpu.HBM)
PARAMS = pltpu.CompilerParams(vmem_limit_bytes=40 * 1024 * 1024)
EXCITE, RESPONSE, TABLE, ROWS = 0, 1024, 1280, 1296


def call(kernel, out_shape, in_specs, name, flops=0, size=1 << 20, scratch=(), aliases=None, params=PARAMS, out_spec=VMEM):
    many = isinstance(out_shape, tuple)
    return pl.pallas_call(
        kernel,
        out_shape=out_shape,
        in_specs=in_specs,
        out_specs=tuple(out_spec for _ in out_shape) if many else out_spec,
        scratch_shapes=list(scratch),
        input_output_aliases=aliases or {},
        compiler_params=params,
        cost_estimate=pl.CostEstimate(flops=flops, bytes_accessed=size, transcendentals=0),
        name=name,
    )


def partner(at, shifted):
    odd = at % 2
    return (at + 1 - 2 * (odd ^ shifted)) % 4


def peer(y, x, d, shifted):
    return (partner(y, shifted) if d & 2 else y), (partner(x, shifted) if d & 1 else x)


A_UP = (0, 1, 0, 1, 0)
B_UP = (1, 0, 0, 1)


def step(value, k, up):
    perm = []
    for z in range(8):
        perm.append((2 * z + up[k - 1], 2 * ((z + 1) % 8) + up[k]))
        perm.append((2 * z + 1 - up[k - 1], 2 * ((z - 1) % 8) + 1 - up[k]))
    return lax.ppermute(value, "group", perm)


def locate(region, me):
    core, kind = me % 2, region % 2
    below = (me // 2 - region // 2) % 8
    slot = jnp.where(kind == core, 0, 8)
    for k in range(1, 5):
        for way, steps in ((0, below), (1, 8 - below)):
            on = A_UP[k] ^ way
            here = (steps == k) & (kind == way)
            slot = jnp.where(here, jnp.where(core == on, k if k < 4 else 7, 8 if k < 4 else 9), slot)
            if k < 4:
                on = B_UP[k] ^ way
                here = (steps == k) & (kind != way)
                slot = jnp.where(here, jnp.where(core == on, 3 + k, 8), slot)
    return slot


def pick_kernel(pair_ref, *refs):
    regions, out_ref = refs[:7], refs[7]
    me = lax.axis_index("group")
    pair = pair_ref[...]
    for n in range(2):
        slot = locate(pair[0, n], me)
        for k, ref in enumerate(regions):

            @pl.when(slot == k)
            def _(ref=ref):
                out_ref[n] = ref[...]


def split3(x):
    first = x.astype(BF)
    rest = x - first.astype(F32)
    second = rest.astype(BF)
    third = (rest - second.astype(F32)).astype(BF)
    return first.astype(F32), second.astype(F32), third.astype(F32)


def prepare_kernel(shapes_ref, omega_ref, damping_ref, own_ref, table_ref):
    own_ref[...] = shapes_ref[:, 0]
    pieces = split3(omega_ref[...]) + split3(damping_ref[...])
    rows = lax.broadcasted_iota(jnp.int32, (16, 128), 0)
    table = jnp.zeros((16, 128), F32)
    for n, piece in enumerate(pieces):
        table = jnp.where(rows == n, piece, table)
    table_ref[...] = table.astype(BF)


def fan_kernel(pair_ref, table_ref, *refs):
    regions, other_ref, far_ref, out_refs, picked_ref = refs[:8], refs[8], refs[9], refs[10:14], refs[14]
    me = lax.axis_index("group")
    pair = pair_ref[...]
    for n in range(2):
        slot = locate(pair[0, n], me)
        for k, ref in enumerate(regions + (other_ref.at[n], far_ref)):

            @pl.when(slot == k)
            def _(ref=ref):
                picked_ref[n] = ref[...]

    core = me % 2
    at_mode = lax.axis_index("mode")
    for d, out_ref in enumerate(out_refs):
        y, x = peer(at_mode // 4, at_mode % 4, d, 1 - core)
        out_ref[EXCITE : EXCITE + 512, :] = picked_ref[1, 0]
        out_ref[EXCITE + 512 : EXCITE + 1024, :] = picked_ref[1, 1]
        for e in range(4):
            owner_y, owner_x = peer(y, x, e, core)
            owned = pl.ds(pl.multiple_of(32 * (4 * owner_y + owner_x), 32), 32)
            at = RESPONSE + 32 * e
            out_ref[at : at + 32, :] = picked_ref[0, 0, owned, :]
            out_ref[at + 128 : at + 160, :] = picked_ref[0, 1, owned, :]
        out_ref[TABLE:ROWS, :] = table_ref[...]


def weights(table, speed):
    omega = table[0:1] + table[1:2] + table[2:3]
    damping = table[3:4] + table[4:5] + table[5:6]
    a = omega * omega - speed * speed
    b = 2.0 * damping * omega * speed
    denom = a * a + b * b
    return a / denom, -b / denom


def share(parts, speeds_ref):
    left, modes = [], []
    for ref in parts:
        res_re = ref[RESPONSE : RESPONSE + 128, :]
        res_im = ref[RESPONSE + 128 : RESPONSE + 256, :]
        left.append(jnp.concatenate([res_re, res_im], axis=0))
        left.append(jnp.concatenate([-res_im, res_re], axis=0))
        modes.append(ref[TABLE:ROWS, :].astype(F32))
    left = jnp.concatenate(left, axis=1)
    for s in range(4):
        right = []
        for ref, table in zip(parts, modes):
            wre, wim = weights(table, speeds_ref[s : s + 1, :])
            ere = ref[EXCITE : EXCITE + 512, :].astype(F32)
            eim = ref[EXCITE + 512 : EXCITE + 1024, :].astype(F32)
            right.append((wre * ere - wim * eim).astype(BF))
            right.append((wre * eim + wim * ere).astype(BF))
        right = jnp.concatenate(right, axis=1)
        yield s, lax.dot_general(
            left, right, (((1,), (1,)), ((), ())), preferred_element_type=F32
        )


def first_kernel(part_ref, speeds_ref, out_ref, speed_rows_ref):
    rows = lax.broadcasted_iota(jnp.int32, (8, 128), 0)
    speeds = jnp.zeros((8, 128), F32)
    for s in range(4):
        speeds = jnp.where(rows == s, speeds_ref[s], speeds)
    speed_rows_ref[...] = speeds
    for s, both in share([part_ref], speed_rows_ref):
        out_ref[s] = both


def next_kernel(total_ref, part_ref, speeds_ref, out_ref):
    for s, both in share([part_ref], speeds_ref):
        out_ref[s] = total_ref[s] + both


def last_kernel(total_ref, part_ref, other_ref, speeds_ref, own_ref, *out_refs):
    parts = (part_ref, other_ref)
    right, modes = [], []
    for ref in parts:
        right.append(ref[EXCITE : EXCITE + 512, :])
        right.append(ref[EXCITE + 512 : EXCITE + 1024, :])
        modes.append(ref[TABLE:ROWS, :].astype(F32))
    right = jnp.concatenate(right, axis=1)
    for s in range(4):
        left = []
        for ref, table in zip(parts, modes):
            wre, wim = weights(table, speeds_ref[s : s + 1, :])
            rre = ref[RESPONSE : RESPONSE + 128, :].astype(F32)
            rim = ref[RESPONSE + 128 : RESPONSE + 256, :].astype(F32)
            lre = wre * rre - wim * rim
            lim = wre * rim + wim * rre
            left.append(jnp.concatenate([lre, lim], axis=0).astype(BF))
            left.append(jnp.concatenate([-lim, lre], axis=0).astype(BF))
        both = total_ref[s] + lax.dot_general(
            jnp.concatenate(left, axis=1),
            right,
            (((1,), (1,)), ((), ())),
            preferred_element_type=F32,
        )
        for c in range(2):
            at = (2 * s + c) * 512
            own_ref[:, at : at + 512] = both[128 * c : 128 * c + 32]
            for e in range(1, 4):
                row = 128 * c + 32 * e
                out_refs[e - 1][:, at : at + 512] = both[row : row + 32].astype(BF)


def sum_kernel(*refs):
    terms, out_ref, total_ref, sems = refs[:4], refs[4], refs[5], refs[6]
    copies = []
    for s in range(4):
        for c in range(2):
            at = (2 * s + c) * 512
            total = terms[0][:, at : at + 512]
            for ref in terms[1:]:
                total = total + ref[:, at : at + 512].astype(F32)
            total_ref[:, s, c, :] = total
        copy = pltpu.make_async_copy(total_ref.at[:, s], out_ref.at[:, 0, s], sems.at[s])
        copy.start()
        copies.append(copy)
    for copy in copies:
        copy.wait()


def exchange(value, d, flip):
    perm = []
    for g in range(16):
        for m in range(16):
            y, x = peer(m // 4, m % 4, d, 1 ^ (g % 2) ^ flip)
            perm.append((16 * g + m, 16 * g + 4 * y + x))
    return lax.ppermute(value, ("group", "mode"), perm)


def swap_cores(value):
    return lax.ppermute(value, "group", [(g, g ^ 1) for g in range(16)])


def shards(shapes, pairs, omega, damping, speeds):
    a1 = step(shapes.reshape(2, 512, 128), 1, A_UP)
    own, table = call(
        prepare_kernel,
        (jax.ShapeDtypeStruct((2, 512, 128), BF), jax.ShapeDtypeStruct((16, 128), BF)),
        [VMEM] * 3,
        "prepare",
    )(shapes, omega.reshape(1, 128), damping.reshape(1, 128))
    b1 = step(own, 1, B_UP)
    a2 = step(a1, 2, A_UP)
    b2 = step(b1, 2, B_UP)
    a3 = step(a2, 3, A_UP)
    b3 = step(b2, 3, B_UP)
    a4 = step(a3, 4, A_UP)
    regions = (own, a1, a2, a3, b1, b2, b3)
    other = jax.ShapeDtypeStruct((2, 2, 512, 128), BF)
    wanted = call(pick_kernel, other, [VMEM] * 8, "pick_regions")(swap_cores(pairs), *regions)
    message = jax.ShapeDtypeStruct((ROWS, 128), BF)
    fanned = call(
        fan_kernel,
        (message,) * 4,
        [VMEM] * 12,
        "fan_out",
        scratch=[pltpu.VMEM((2, 2, 512, 128), BF)],
    )(pairs, table, *regions, a4, swap_cores(wanted), swap_cores(a4))
    parts = [fanned[0]] + [exchange(fanned[d], d, 0) for d in (3, 1, 2)]
    sums = jax.ShapeDtypeStruct((4, 256, 512), F32)
    total, speed_rows = call(
        first_kernel,
        (sums, jax.ShapeDtypeStruct((8, 128), F32)),
        [VMEM, SMEM],
        "product_0",
        flops=1 << 28,
    )(parts[0], speeds)
    total = call(
        next_kernel, sums, [VMEM] * 3, "product_1", flops=1 << 28, aliases={0: 0}
    )(total, parts[1], speed_rows)
    block = jax.ShapeDtypeStruct((32, 4096), BF)
    made = call(
        last_kernel,
        (jax.ShapeDtypeStruct((32, 4096), F32), block, block, block),
        [VMEM] * 4,
        "product_2",
        flops=1 << 29,
    )(total, parts[2], parts[3], speed_rows)
    terms = [made[0]] + [exchange(made[e], e, 1) for e in (3, 2, 1)]
    return call(
        sum_kernel,
        jax.ShapeDtypeStruct((32, 1, 4, 2, 512), F32),
        [VMEM] * 4,
        "sum_terms",
        scratch=[pltpu.VMEM((32, 4, 2, 512), F32), pltpu.SemaphoreType.DMA((4,))],
        out_spec=HBM,
    )(*terms)


def solution(mesh):
    in_specs = (P(None, "group", None, "mode"), P("group", None), P("mode"), P("mode"), P())
    out_specs = P("mode", "group", None, None, None)
    return jax.shard_map(shards, mesh=mesh, in_specs=in_specs, out_specs=out_specs, check_vma=False)
```
